32 devices in a mesh: dom: 16 (over z, y, x), rep: 2 (over core).
Axes of the slice: x: 2, y: 2, z: 4, core: 2. Of those that a mesh axis runs over, the one named last changes fastest.
Arguments:
- features: bfloat16 [131072, 256], P('dom'), may hold values from -6 to 6
- node_order: int32 [16, 8192], P('dom'), may hold values from 0 to 8191, each once within a row
- section_owner: int32 [4], replicated, may hold values from 0 to 15, as said below
- send_blocks: int32 [4, 32], replicated, may hold values from 0 to 63, as said below
- tile_rows: int32 [16, 4, 32], P('dom', None, 'rep'), may hold values from 0 to 63
- tile_cols: int32 [16, 4, 32], P('dom', None, 'rep'), may hold values from 0 to 31
- tiles: bfloat16 [16, 4, 32, 128, 128], P('dom', None, 'rep'), may hold values from -0.375 to 0.375
- weight: bfloat16 [256, 256], replicated, may hold values from -0.375 to 0.375
Outputs:
- hidden: bfloat16 [131072, 256], P(('dom', 'rep'))
The draws below stay inside these ranges and needn't reach their ends.
Inputs may be any that keep to these rules, and one draw needn't show every extreme that they name: `section_owner`: 4 different partitions; partitions 0 and 15 are always among them. `send_blocks`: each row holds 32 different block numbers in rising order, always including 0 and 63.
All inputs are finite; a program needn't handle non-finite values.
Results may differ from the reference program's by a relative error of at most 0.014.
Values may be sent and summed in bfloat16 or wider, within the bound.
No kernel may reach another device: no remote copies, remote signals or barrier semaphores. Data moves between devices by JAX's collectives and lax.ppermute only.
A program may use at most 64 MiB of HBM per device.

```python
import jax
import jax.numpy as jnp
from jax import lax

F = 256
TILE = 128
NB = 64
SB = 32
KR = 16
SECTIONS = 4
K = 32
NODES = 131072
N_DOM = 16
N_REP = 2


def draw_section_owner(key, part):
    first_key = jax.random.fold_in(key, 11)
    second_key = jax.random.fold_in(key, 12)
    middle = jax.random.permutation(first_key, N_DOM - 2)[:SECTIONS - 2].astype(jnp.int32) + 1
    chosen = jnp.concatenate([jnp.array([0, N_DOM - 1], dtype=jnp.int32), middle])
    placed = jax.random.permutation(second_key, SECTIONS)
    return chosen[placed].astype(jnp.int32)


def draw_send_blocks(key, part):
    keys = jax.random.split(jax.random.fold_in(key, 21), SECTIONS)

    def one_row(row_key):
        middle = jax.random.permutation(row_key, NB - 2)[:SB - 2].astype(jnp.int32) + 1
        ends = jnp.array([0, NB - 1], dtype=jnp.int32)
        return jnp.sort(jnp.concatenate([ends, middle]))
    return jax.vmap(one_row)(keys).astype(jnp.int32)


def set_ends(entries, key, least, top_value):
    extent = entries.shape
    place = [jax.random.randint(jax.random.fold_in(key, axis), (), 0, extent[axis]) for axis in range(len(extent))]
    entries = entries.at[tuple(place)].set(least)
    longest = extent.index(max(extent))
    place[longest] = (place[longest] + 1) % extent[longest]
    return entries.at[tuple(place)].set(top_value)


def levels(own_key, extent, shards, smallest, largest):
    def one(position, blocks):
        heights = jax.random.uniform(jax.random.fold_in(jax.random.fold_in(own_key, 6), position), (blocks,), jnp.float32, smallest / len(shards), largest / len(shards))
        return jnp.repeat(jnp.exp(heights), extent[position] // blocks).reshape((-1,) + (1,) * (len(extent) - position - 1))

    loudness = one(*shards[0])
    for cut in shards[1:]:
        loudness = loudness * one(*cut)
    return loudness


def scatter_about(key, shape, spread, reach, pieces=(), held_as=jnp.bfloat16):
    gain = levels(key, shape, pieces, -0.22, 0.18) if pieces else 1.0
    entries = jax.random.normal(key, shape, jnp.float32) * spread * gain
    return jnp.minimum(jnp.maximum(entries, -reach), reach).astype(held_as)


def setup_inputs(seed: int = 0) -> dict:
    arg_keys = jax.random.split(jax.random.key(seed), 9)
    return {
        "features": scatter_about(arg_keys[0], (NODES, F), 1.0, 6.0, ((0, 16),)),
        "node_order": jax.vmap(lambda own: jax.random.permutation(own, NB * TILE))(jax.random.split(arg_keys[1], N_DOM)).reshape((N_DOM, NB * TILE)).astype(jnp.int32),
        "section_owner": draw_section_owner(jax.random.fold_in(arg_keys[8], 71), 0),
        "send_blocks": draw_send_blocks(jax.random.fold_in(arg_keys[8], 71), 0),
        "tile_rows": set_ends(jax.random.randint(arg_keys[4], (N_DOM, SECTIONS, K), 0, NB), jax.random.fold_in(arg_keys[4], 1), 0, NB - 1).astype(jnp.int32),
        "tile_cols": set_ends(jax.random.randint(arg_keys[5], (N_DOM, SECTIONS, K), 0, SB), jax.random.fold_in(arg_keys[5], 1), 0, SB - 1).astype(jnp.int32),
        "tiles": scatter_about(arg_keys[6], (N_DOM, SECTIONS, K, TILE, TILE), (TILE * SECTIONS * K // NB) ** -0.5, 0.375, ((0, 16), (2, 2))),
        "weight": scatter_about(arg_keys[7], (F, F), F ** -0.5, 0.375),
    }


def reference(features, node_order, section_owner, send_blocks, tile_rows, tile_cols, tiles, weight):
    grouped = features.reshape(N_DOM, NB * TILE, F)
    curve = jax.vmap(lambda block, order: jnp.take(block, order, axis=0))(grouped, node_order)
    curve = curve.reshape(N_DOM, NB, TILE, F)
    sent = jnp.stack([jnp.take(curve[section_owner[s]], send_blocks[s], axis=0) for s in range(SECTIONS)])
    block_ids = jnp.arange(NB, dtype=jnp.int32)

    def partition(packed):
        rows, cols, tiled = packed
        total = jnp.zeros((N_REP, NB, TILE, F), jnp.float32)
        for s in range(SECTIONS):
            chosen = jnp.take(sent[s], cols[s], axis=0).astype(jnp.float32)
            product = jnp.einsum('kij,kjf->kif', tiled[s].astype(jnp.float32), chosen, precision=lax.Precision.HIGHEST)
            onehot = (rows[s][:, None] == block_ids[None, :]).astype(jnp.float32).reshape(N_REP, KR, NB)
            total = total + jnp.einsum('gkn,gkif->gnif', onehot, product.reshape(N_REP, KR, TILE, F), precision=lax.Precision.HIGHEST)
        rounded = lax.optimization_barrier(total.astype(jnp.bfloat16))
        aggregate = jnp.sum(rounded.astype(jnp.float32), axis=0).astype(jnp.bfloat16).reshape(NB * TILE, F)
        mixed = jnp.dot(aggregate, weight, preferred_element_type=jnp.float32)
        return jnp.maximum(mixed, 0.0).astype(jnp.bfloat16)

    result = lax.map(partition, (tile_rows, tile_cols, tiles))
    return result.reshape(NODES, F)
```

```python
import functools

import jax
import jax.numpy as jnp
from jax import lax
from jax.experimental import pallas as pl
from jax.experimental.pallas import tpu as pltpu
from jax.sharding import PartitionSpec as P


def kernel(places, tile_parts, rows_ref, cols_ref, *refs):
    n_pieces = len(places)
    pieces = refs[:n_pieces]
    tile_refs = refs[n_pieces : n_pieces + tile_parts]
    weight_ref, out_ref = refs[n_pieces + tile_parts : n_pieces + tile_parts + 2]
    sent, tiles, acc, stage, mine, sem, tile_sem, out_sem = refs[n_pieces + tile_parts + 2 :]
    n_tiles = rows_ref.shape[0]
    tile_len = tiles.shape[1]
    n_blocks = acc.shape[0]

    copies = []
    for i, place in enumerate(places):
        count = pieces[i].shape[0]
        copies.append(
            pltpu.make_async_copy(pieces[i], sent.at[pl.ds(place, count)], sem.at[i])
        )
    per = n_tiles // tile_parts
    for i in range(tile_parts):
        copies.append(
            pltpu.make_async_copy(tile_refs[i], tiles.at[pl.ds(i * per, per)], tile_sem.at[i])
        )
    for copy in copies:
        copy.start()

    acc[...] = jnp.zeros_like(acc)

    def pick(t, count):
        here = jnp.logical_and(rows_ref[t] >= 0, rows_ref[t] < n_blocks)

        @pl.when(here)
        def _():
            mine[count] = t

        return count + here.astype(jnp.int32)

    n_mine = lax.fori_loop(0, n_tiles, pick, jnp.int32(0))

    for copy in copies:
        copy.wait()

    def step(i, carry):
        t = mine[i]
        acc[rows_ref[t]] += jnp.dot(
            tiles[t], sent[cols_ref[t]], preferred_element_type=jnp.float32
        )
        return carry

    lax.fori_loop(0, n_mine, step, 0)

    group = stage.shape[1]
    steps = n_blocks // group
    outs = []
    for i in range(steps):
        if i >= 2:
            outs[i - 2].wait()
        total = acc[pl.ds(i * group, group)].reshape(group * tile_len, acc.shape[2])
        mixed = jnp.dot(
            total.astype(jnp.bfloat16), weight_ref[...], preferred_element_type=jnp.float32
        )
        stage[i % 2] = (
            jnp.maximum(mixed, 0.0).astype(out_ref.dtype).reshape(stage.shape[1:])
        )
        copy = pltpu.make_async_copy(
            stage.at[i % 2], out_ref.at[pl.ds(i * group, group)], out_sem.at[i % 2]
        )
        copy.start()
        outs.append(copy)
    for copy in outs[max(steps - 2, 0) :]:
        copy.wait()


def products(pieces, places, tile_list, rows, cols, weight, n_sent, n_blocks):
    tile_len = tile_list[0].shape[1]
    width = weight.shape[0]
    n_tiles = rows.shape[0]
    group = min(4, n_blocks)
    any_spec = pl.BlockSpec(memory_space=pl.ANY)
    smem = pl.BlockSpec(memory_space=pltpu.SMEM)
    return pl.pallas_call(
        functools.partial(kernel, tuple(places), len(tile_list)),
        out_shape=jax.ShapeDtypeStruct((n_blocks, tile_len, weight.shape[1]), jnp.bfloat16),
        in_specs=[smem, smem]
        + [any_spec] * (len(pieces) + len(tile_list))
        + [pl.BlockSpec(memory_space=pltpu.VMEM)],
        out_specs=any_spec,
        scratch_shapes=[
            pltpu.VMEM((n_sent, tile_len, width), jnp.bfloat16),
            pltpu.VMEM((n_tiles, tile_len, tile_len), jnp.bfloat16),
            pltpu.VMEM((n_blocks, tile_len, width), jnp.float32),
            pltpu.VMEM((2, group, tile_len, weight.shape[1]), jnp.bfloat16),
            pltpu.SMEM((n_tiles,), jnp.int32),
            pltpu.SemaphoreType.DMA((len(pieces),)),
            pltpu.SemaphoreType.DMA((len(tile_list),)),
            pltpu.SemaphoreType.DMA((2,)),
        ],
        compiler_params=pltpu.CompilerParams(vmem_limit_bytes=40 * 1024 * 1024),
        cost_estimate=pl.CostEstimate(
            flops=2 * n_tiles * tile_len * tile_len * width, bytes_accessed=16 << 20, transcendentals=0
        ),
    )(rows, cols, *pieces, *tile_list, weight)


def candidate(features, node_order, section_owner, send_blocks, tile_len):
    me = lax.axis_index("dom")
    section = jnp.argmax(section_owner == me)
    share = send_blocks.shape[1] // lax.axis_size("rep")
    picks = lax.dynamic_slice(
        send_blocks, (section, lax.axis_index("rep") * share), (1, share)
    )[0]
    order = node_order[0].reshape(-1, tile_len)
    rows = order.at[picks].get(mode="promise_in_bounds").reshape(-1)
    return features.at[rows].get(mode="promise_in_bounds")


def gather_small(shard):
    sections = shard.shape[0]
    ring = {
        k: [(z * 4 + q, ((z - k) % 4) * 4 + q) for z in range(4) for q in range(4)]
        for k in (1, 2, 3)
    }
    flip = {k: [(i, i ^ k) for i in range(16)] for k in (1, 2)}

    def move(value, pairs):
        return lax.ppermute(value, "dom", pairs)

    shifted = [shard] + [move(shard, ring[k]) for k in (1, 2, 3)]
    pieces = list(shifted)
    places = [k * sections for k in range(4)]
    for first in (0, 2):
        pair = jnp.concatenate(shifted[first : first + 2])
        by_x = move(pair, flip[1])
        by_y = move(pair, flip[2])
        pieces += [by_x, by_y, move(by_x[:sections], flip[2]), move(by_y[sections:], flip[1])]
        places += [
            (4 + first) * sections,
            (8 + first) * sections,
            (12 + first) * sections,
            (13 + first) * sections,
        ]
    return pieces, places


def body(features, node_order, section_owner, send_blocks, tile_rows, tile_cols, tiles, weight):
    width = features.shape[1]
    tile_len = tiles.shape[3]
    blocks = features.shape[0] // tile_len
    n_dom, n_rep = lax.axis_size("dom"), lax.axis_size("rep")
    sections, n_send = send_blocks.shape
    me, rep = lax.axis_index("dom"), lax.axis_index("rep")
    n_blocks = blocks // n_rep
    small = n_dom == 16 and n_rep == 2 and n_send == n_dom * n_rep

    own_tiles = tiles[0].reshape(-1, tile_len, tile_len)
    numbers = jnp.stack([tile_rows[0], tile_cols[0]])
    section_of = jnp.broadcast_to(jnp.arange(sections)[:, None], tile_rows.shape[1:])
    if small:
        swap = [(0, 1), (1, 0)]
        tile_list = [own_tiles, lax.ppermute(own_tiles, "rep", swap)]
        numbers = jnp.stack([numbers, lax.ppermute(numbers, "rep", swap)])
    else:
        tile_list = [lax.all_gather(own_tiles, "rep", axis=0, tiled=True)]
        numbers = lax.all_gather(numbers, "rep", axis=0)
    rows = (numbers[:, 0] - rep * n_blocks).reshape(-1)
    cols = numbers[:, 1]

    mine = candidate(features, node_order, section_owner, send_blocks, tile_len)
    landed = lax.all_to_all(mine, "dom", 0, 0, tiled=True)
    landed = landed.reshape(n_dom, -1, width)
    shard = landed.at[section_owner].get(mode="promise_in_bounds")

    if small:
        pieces, places = gather_small(shard)
        half = n_dom * sections
        pieces = pieces + [lax.ppermute(piece, "rep", swap) for piece in pieces]
        places = places + [half + place for place in places]
        source = cols % n_dom
        other = (cols // n_dom != rep).astype(jnp.int32)
        across = (source ^ me) & 3
        shift = (source // 4 - me // 4) & 3
        slots = ((other * 4 + across) * 4 + shift) * sections + section_of
    else:
        whole = lax.all_gather(shard, ("rep", "dom"), axis=0)
        whole = whole.transpose(1, 0, 2, 3).reshape(sections * n_send, tile_len, width)
        pieces, places = [whole], [0]
        slots = section_of * n_send + cols
    hidden = products(
        pieces, places, tile_list, rows, slots.reshape(-1), weight, sections * n_send, n_blocks
    )
    return hidden.reshape(n_blocks * tile_len, -1)


def solution(mesh):
    return jax.shard_map(
        body,
        mesh=mesh,
        in_specs=(
            P("dom", None),
            P("dom", None),
            P(),
            P(),
            P("dom", None, "rep"),
            P("dom", None, "rep"),
            P("dom", None, "rep", None, None),
            P(),
        ),
        out_specs=P(("dom", "rep"), None),
        check_vma=False,
    )
```

```python
import functools

import jax
import jax.numpy as jnp
from jax import lax
from jax.experimental import pallas as pl
from jax.experimental.pallas import tpu as pltpu
from jax.sharding import PartitionSpec as P


def kernel(places, tile_parts, rows_ref, cols_ref, *refs):
    n_pieces = len(places)
    pieces = refs[:n_pieces]
    tile_refs = refs[n_pieces : n_pieces + tile_parts]
    weight_ref, out_ref = refs[n_pieces + tile_parts : n_pieces + tile_parts + 2]
    sent, tiles, acc, stage, mine, sem, tile_sem, out_sem = refs[n_pieces + tile_parts + 2 :]
    n_tiles = rows_ref.shape[0]
    tile_len = tiles.shape[1]
    n_blocks = acc.shape[0]

    copies = []
    for i, place in enumerate(places):
        count = pieces[i].shape[0]
        copies.append(
            pltpu.make_async_copy(pieces[i], sent.at[pl.ds(place, count)], sem.at[i])
        )
    per = n_tiles // tile_parts
    for i in range(tile_parts):
        copies.append(
            pltpu.make_async_copy(tile_refs[i], tiles.at[pl.ds(i * per, per)], tile_sem.at[i])
        )
    for copy in copies:
        copy.start()

    acc[...] = jnp.zeros_like(acc)

    def pick(t, count):
        here = jnp.logical_and(rows_ref[t] >= 0, rows_ref[t] < n_blocks)

        @pl.when(here)
        def _():
            mine[count] = t

        return count + here.astype(jnp.int32)

    n_mine = lax.fori_loop(0, n_tiles, pick, jnp.int32(0))

    for copy in copies:
        copy.wait()

    def step(i, carry):
        t = mine[i]
        acc[rows_ref[t]] += jnp.dot(
            tiles[t], sent[cols_ref[t]], preferred_element_type=jnp.float32
        )
        return carry

    lax.fori_loop(0, n_mine, step, 0)

    group = stage.shape[1]
    steps = n_blocks // group
    outs = []
    for i in range(steps):
        if i >= 2:
            outs[i - 2].wait()
        total = acc[pl.ds(i * group, group)].reshape(group * tile_len, acc.shape[2])
        mixed = jnp.dot(
            total.astype(jnp.bfloat16), weight_ref[...], preferred_element_type=jnp.float32
        )
        stage[i % 2] = (
            jnp.maximum(mixed, 0.0).astype(out_ref.dtype).reshape(stage.shape[1:])
        )
        copy = pltpu.make_async_copy(
            stage.at[i % 2], out_ref.at[pl.ds(i * group, group)], out_sem.at[i % 2]
        )
        copy.start()
        outs.append(copy)
    for copy in outs[max(steps - 2, 0) :]:
        copy.wait()


def products(pieces, places, tile_list, rows, cols, weight, n_sent, n_blocks):
    tile_len = tile_list[0].shape[1]
    width = weight.shape[0]
    n_tiles = rows.shape[0]
    group = min(4, n_blocks)
    any_spec = pl.BlockSpec(memory_space=pltpu.HBM)
    smem = pl.BlockSpec(memory_space=pltpu.SMEM)
    return pl.pallas_call(
        functools.partial(kernel, tuple(places), len(tile_list)),
        out_shape=jax.ShapeDtypeStruct((n_blocks, tile_len, weight.shape[1]), jnp.bfloat16),
        in_specs=[smem, smem]
        + [any_spec] * (len(pieces) + len(tile_list))
        + [pl.BlockSpec(memory_space=pltpu.VMEM)],
        out_specs=any_spec,
        scratch_shapes=[
            pltpu.VMEM((n_sent, tile_len, width), jnp.bfloat16),
            pltpu.VMEM((n_tiles, tile_len, tile_len), jnp.bfloat16),
            pltpu.VMEM((n_blocks, tile_len, width), jnp.float32),
            pltpu.VMEM((2, group, tile_len, weight.shape[1]), jnp.bfloat16),
            pltpu.SMEM((n_tiles,), jnp.int32),
            pltpu.SemaphoreType.DMA((len(pieces),)),
            pltpu.SemaphoreType.DMA((len(tile_list),)),
            pltpu.SemaphoreType.DMA((2,)),
        ],
        compiler_params=pltpu.CompilerParams(vmem_limit_bytes=40 * 1024 * 1024),
        cost_estimate=pl.CostEstimate(
            flops=2 * n_tiles * tile_len * tile_len * width, bytes_accessed=16 << 20, transcendentals=0
        ),
    )(rows, cols, *pieces, *tile_list, weight)


def share_rows(node_order, section_owner, send_blocks, tile_len):
    me = lax.axis_index("dom")
    sections, n_send = send_blocks.shape
    mine = (section_owner == me).astype(jnp.int32)
    section = jnp.sum(mine * jnp.arange(sections, dtype=jnp.int32))
    share = n_send // lax.axis_size("rep")
    picks = lax.dynamic_slice(
        send_blocks, (section, lax.axis_index("rep") * share), (1, share)
    )[0]
    order = node_order[0].reshape(-1, tile_len)
    return order.at[picks].get(mode="promise_in_bounds")


def move(value, pairs):
    return lax.ppermute(value, "dom", pairs)


def flip(bits):
    return [(i, i ^ bits) for i in range(16)]


def quad_scatter(features, lines):
    quad = lax.axis_index("dom") % 4
    each = lines.shape[0] // 4
    held = [None] * 4
    for e in (3, 1, 2, 0):
        own = lax.dynamic_slice_in_dim(lines, (quad ^ e) * each, each)
        rows = features.at[own.reshape(-1)].get(mode="promise_in_bounds")
        held[e] = rows.reshape(each, lines.shape[1], features.shape[1])
        if e:
            held[e] = move(held[e], flip(e))
    return held


def along_z(first, at, z, pair):
    middle = [(i, i + 4) for i in range(4, 8)] + [(i, i - 4) for i in range(8, 12)]
    outer = [(i, i - 4) for i in range(4, 8)] + [(i, i + 4) for i in range(8, 12)]
    near = move(first, pair)
    known = jnp.where(at == z, first, near)
    across = move(known, middle)
    beyond = move(across, outer)
    inner = jnp.logical_or(z == 1, z == 2)
    return known, jnp.where(inner, across, beyond)


def quad_gather(own):
    half = own.shape[0] // 2
    by_x = move(own, flip(1))
    by_y = move(own, flip(2))
    return [own, by_x, by_y, move(by_x[:half], flip(2)), move(by_y[half:], flip(1))]


def gather_small(features, lines, section_owner):
    me = lax.axis_index("dom")
    quad, z = me % 4, me // 4
    held = quad_scatter(features, lines)
    is_first, is_last = section_owner == 0, section_owner == 15
    other = jnp.logical_not(jnp.logical_or(is_first, is_last))
    rank = jnp.cumsum(other.astype(jnp.int32)) - 1
    owners = [
        jnp.sum(jnp.where(jnp.logical_and(other, rank == i), section_owner, 0)) for i in (0, 1)
    ]
    low = z < 2
    slot = jnp.where(other, 2 + rank, jnp.where(is_first == low, 0, 1))

    def of(source):
        return lax.select_n(quad ^ source, *held)

    end = jnp.where(low, 0, 3)
    inward = [(i, i + 4) for i in range(4)] + [(i, i - 4) for i in range(12, 16)]
    near, far = along_z(of(end), end, z, inward)
    quarters = [near, far]
    for owner in owners:
        known, rest = along_z(of(owner % 4), owner // 4, z, flip(4))
        quarters.append(jnp.where((owner // 8) == (z // 2), known, rest))
    pieces, places = [], []
    each = near.shape[0]
    for i, quarter in enumerate(quarters):
        pieces += quad_gather(quarter)
        places += [(i * 4 + e) * each for e in range(4)] + [(i * 4 + 3) * each + each // 2]
    return pieces, places, slot


def body(features, node_order, section_owner, send_blocks, tile_rows, tile_cols, tiles, weight):
    width = features.shape[1]
    tile_len = tiles.shape[3]
    blocks = features.shape[0] // tile_len
    n_dom, n_rep = lax.axis_size("dom"), lax.axis_size("rep")
    sections, n_send = send_blocks.shape
    me, rep = lax.axis_index("dom"), lax.axis_index("rep")
    n_blocks = blocks // n_rep
    small = n_dom == 16 and n_rep == 2 and n_send == n_dom * n_rep

    own_tiles = tiles[0].reshape(-1, tile_len, tile_len)
    numbers = jnp.stack([tile_rows[0], tile_cols[0]])
    if small:
        swap = [(0, 1), (1, 0)]
        tile_list = [own_tiles, lax.ppermute(own_tiles, "rep", swap)]
        numbers = jnp.stack([numbers, lax.ppermute(numbers, "rep", swap)])
    else:
        tile_list = [lax.all_gather(own_tiles, "rep", axis=0, tiled=True)]
        numbers = lax.all_gather(numbers, "rep", axis=0)
    rows = (numbers[:, 0] - rep * n_blocks).reshape(-1)
    cols = numbers[:, 1]

    lines = share_rows(node_order, section_owner, send_blocks, tile_len)
    if small:
        pieces, places, slot = gather_small(features, lines, section_owner)
        half = sections * n_send // 2
        pieces = pieces + [lax.ppermute(piece, "rep", swap) for piece in pieces]
        places = places + [half + place for place in places]
        block = cols % n_dom
        across = (block // 4) ^ (me % 4)
        other = (cols // n_dom != rep).astype(jnp.int32)
        slots = ((other * sections + slot[:, None]) * 4 + across) * 4 + block % 4
    else:
        mine = features.at[lines.reshape(-1)].get(mode="promise_in_bounds")
        landed = lax.all_to_all(mine, "dom", 0, 0, tiled=True)
        landed = landed.reshape(n_dom, -1, width)
        shard = landed.at[section_owner].get(mode="promise_in_bounds")
        whole = lax.all_gather(shard, ("rep", "dom"), axis=0)
        whole = whole.transpose(1, 0, 2, 3).reshape(sections * n_send, tile_len, width)
        pieces, places = [whole], [0]
        slots = jnp.arange(sections)[:, None] * n_send + cols
    hidden = products(
        pieces, places, tile_list, rows, slots.reshape(-1), weight, sections * n_send, n_blocks
    )
    return hidden.reshape(n_blocks * tile_len, -1)


def solution(mesh):
    return jax.shard_map(
        body,
        mesh=mesh,
        in_specs=(
            P("dom", None),
            P("dom", None),
            P(),
            P(),
            P("dom", None, "rep"),
            P("dom", None, "rep"),
            P("dom", None, "rep", None, None),
            P(),
        ),
        out_specs=P(("dom", "rep"), None),
        check_vma=False,
    )
```

```python
import functools

import jax
import jax.numpy as jnp
from jax import lax
from jax.experimental import pallas as pl
from jax.experimental.pallas import tpu as pltpu
from jax.sharding import PartitionSpec as P


def kernel(places, tile_parts, rows_ref, cols_ref, *refs):
    n_pieces = len(places)
    pieces = refs[:n_pieces]
    tile_refs = refs[n_pieces : n_pieces + tile_parts]
    weight_ref, out_ref = refs[n_pieces + tile_parts : n_pieces + tile_parts + 2]
    sent, tiles, acc, stage, mine, sem, tile_sem, out_sem = refs[n_pieces + tile_parts + 2 :]
    n_tiles = rows_ref.shape[0]
    tile_len = tiles.shape[1]
    n_blocks = acc.shape[0]

    copies = []
    for i, place in enumerate(places):
        count = pieces[i].shape[0]
        copies.append(
            pltpu.make_async_copy(pieces[i], sent.at[pl.ds(place, count)], sem.at[i])
        )
    per = n_tiles // tile_parts
    for i in range(tile_parts):
        copies.append(
            pltpu.make_async_copy(tile_refs[i], tiles.at[pl.ds(i * per, per)], tile_sem.at[i])
        )
    for copy in copies:
        copy.start()

    acc[...] = jnp.zeros_like(acc)

    def pick(t, count):
        here = jnp.logical_and(rows_ref[t] >= 0, rows_ref[t] < n_blocks)

        @pl.when(here)
        def _():
            mine[count] = t

        return count + here.astype(jnp.int32)

    n_mine = lax.fori_loop(0, n_tiles, pick, jnp.int32(0))

    for copy in copies:
        copy.wait()

    def step(i, carry):
        t = mine[i]
        acc[rows_ref[t]] += jnp.dot(
            tiles[t], sent[cols_ref[t]], preferred_element_type=jnp.float32
        )
        return carry

    lax.fori_loop(0, n_mine, step, 0)

    group = stage.shape[1]
    steps = n_blocks // group
    outs = []
    for i in range(steps):
        if i >= 2:
            outs[i - 2].wait()
        total = acc[pl.ds(i * group, group)].reshape(group * tile_len, acc.shape[2])
        mixed = jnp.dot(
            total.astype(jnp.bfloat16), weight_ref[...], preferred_element_type=jnp.float32
        )
        stage[i % 2] = (
            jnp.maximum(mixed, 0.0).astype(out_ref.dtype).reshape(stage.shape[1:])
        )
        copy = pltpu.make_async_copy(
            stage.at[i % 2], out_ref.at[pl.ds(i * group, group)], out_sem.at[i % 2]
        )
        copy.start()
        outs.append(copy)
    for copy in outs[max(steps - 2, 0) :]:
        copy.wait()


def products(pieces, places, tile_list, rows, cols, weight, n_sent, n_blocks):
    tile_len = tile_list[0].shape[1]
    width = weight.shape[0]
    n_tiles = rows.shape[0]
    group = min(4, n_blocks)
    any_spec = pl.BlockSpec(memory_space=pltpu.HBM)
    smem = pl.BlockSpec(memory_space=pltpu.SMEM)
    return pl.pallas_call(
        functools.partial(kernel, tuple(places), len(tile_list)),
        out_shape=jax.ShapeDtypeStruct((n_blocks, tile_len, weight.shape[1]), jnp.bfloat16),
        in_specs=[smem, smem]
        + [any_spec] * (len(pieces) + len(tile_list))
        + [pl.BlockSpec(memory_space=pltpu.VMEM)],
        out_specs=any_spec,
        scratch_shapes=[
            pltpu.VMEM((n_sent, tile_len, width), jnp.bfloat16),
            pltpu.VMEM((n_tiles, tile_len, tile_len), jnp.bfloat16),
            pltpu.VMEM((n_blocks, tile_len, width), jnp.float32),
            pltpu.VMEM((2, group, tile_len, weight.shape[1]), jnp.bfloat16),
            pltpu.SMEM((n_tiles,), jnp.int32),
            pltpu.SemaphoreType.DMA((len(pieces),)),
            pltpu.SemaphoreType.DMA((len(tile_list),)),
            pltpu.SemaphoreType.DMA((2,)),
        ],
        compiler_params=pltpu.CompilerParams(vmem_limit_bytes=60 * 1024 * 1024),
        cost_estimate=pl.CostEstimate(
            flops=2 * n_tiles * tile_len * tile_len * width, bytes_accessed=16 << 20, transcendentals=0
        ),
    )(rows, cols, *pieces, *tile_list, weight)


def share_rows(node_order, section_owner, send_blocks, tile_len):
    me = lax.axis_index("dom")
    sections, n_send = send_blocks.shape
    mine = (section_owner == me).astype(jnp.int32)
    section = jnp.sum(mine * jnp.arange(sections, dtype=jnp.int32))
    share = n_send // lax.axis_size("rep")
    picks = lax.dynamic_slice(
        send_blocks, (section, lax.axis_index("rep") * share), (1, share)
    )[0]
    order = node_order[0].reshape(-1, tile_len)
    return order.at[picks].get(mode="promise_in_bounds")


def move(value, pairs):
    return lax.ppermute(value, "dom", pairs)


def flip(bits):
    return [(i, i ^ bits) for i in range(16)]


def cross(value, turn):
    pairs = []
    for i in range(16):
        for core in (0, 1):
            pairs.append((2 * i + core, 2 * (i ^ (1 if core == turn else 2)) + core))
    return lax.ppermute(value, ("dom", "rep"), pairs)


def place_of(across, core):
    return jnp.where(core == 0, across, (across & 1) * 2 + across // 2)


def quad_scatter(features, lines):
    quad, rep = lax.axis_index("dom") % 4, lax.axis_index("rep")
    first, second = 1 + rep, 2 - rep
    each = lines.shape[0] // 4

    def rows(*across):
        own = [lax.dynamic_slice_in_dim(lines, (quad ^ e) * each, each) for e in across]
        taken = features.at[jnp.concatenate(own).reshape(-1)].get(mode="promise_in_bounds")
        return taken.reshape(2 * each, lines.shape[1], features.shape[1])

    by_first = cross(rows(3, first), 0)
    kept = rows(second, 0)
    by_second = cross(jnp.concatenate([kept[:each], by_first[:each]]), 1)
    return kept[each:], by_first[each:], by_second[:each], by_second[each:]


def along_z(first, at, z, pair):
    middle = [(i, i + 4) for i in range(4, 8)] + [(i, i - 4) for i in range(8, 12)]
    outer = [(i, i - 4) for i in range(4, 8)] + [(i, i + 4) for i in range(8, 12)]
    near = move(first, pair)
    known = jnp.where(at == z, first, near)
    across = move(known, middle)
    beyond = move(across, outer)
    inner = jnp.logical_or(z == 1, z == 2)
    return known, jnp.where(inner, across, beyond)


def quad_gather(own):
    pair = jnp.concatenate([own, cross(own, 0)])
    return [pair, cross(pair, 1)]


def gather_small(features, lines, section_owner):
    me = lax.axis_index("dom")
    quad, z = me % 4, me // 4
    held = quad_scatter(features, lines)
    is_first, is_last = section_owner == 0, section_owner == 15
    other = jnp.logical_not(jnp.logical_or(is_first, is_last))
    rank = jnp.cumsum(other.astype(jnp.int32)) - 1
    owners = [
        jnp.sum(jnp.where(jnp.logical_and(other, rank == i), section_owner, 0)) for i in (0, 1)
    ]
    low = z < 2
    slot = jnp.where(other, 2 + rank, jnp.where(is_first == low, 0, 1))

    def of(source):
        return lax.select_n(place_of(quad ^ source, lax.axis_index("rep")), *held)

    end = jnp.where(low, 0, 3)
    inward = [(i, i + 4) for i in range(4)] + [(i, i - 4) for i in range(12, 16)]
    quarters = list(along_z(of(end), end, z, inward))
    for owner in owners:
        known, rest = along_z(of(owner % 4), owner // 4, z, flip(4))
        quarters.append(jnp.where((owner // 8) == (z // 2), known, rest))
    pieces, places = [], []
    each = quarters[0].shape[0]
    for i, quarter in enumerate(quarters):
        pieces += quad_gather(quarter)
        places += [i * 4 * each, (i * 4 + 2) * each]
    return pieces, places, slot


def body(features, node_order, section_owner, send_blocks, tile_rows, tile_cols, tiles, weight):
    width = features.shape[1]
    tile_len = tiles.shape[3]
    blocks = features.shape[0] // tile_len
    n_dom, n_rep = lax.axis_size("dom"), lax.axis_size("rep")
    sections, n_send = send_blocks.shape
    me, rep = lax.axis_index("dom"), lax.axis_index("rep")
    n_blocks = blocks // n_rep
    small = n_dom == 16 and n_rep == 2 and n_send == n_dom * n_rep

    own_tiles = tiles[0].reshape(-1, tile_len, tile_len)
    numbers = jnp.stack([tile_rows[0], tile_cols[0]])
    if small:
        swap = [(0, 1), (1, 0)]
        tile_list = [own_tiles, lax.ppermute(own_tiles, "rep", swap)]
        numbers = jnp.stack([numbers, lax.ppermute(numbers, "rep", swap)])
    else:
        tile_list = [lax.all_gather(own_tiles, "rep", axis=0, tiled=True)]
        numbers = lax.all_gather(numbers, "rep", axis=0)
    rows = (numbers[:, 0] - rep * n_blocks).reshape(-1)
    cols = numbers[:, 1]

    lines = share_rows(node_order, section_owner, send_blocks, tile_len)
    if small:
        pieces, places, slot = gather_small(features, lines, section_owner)
        half = sections * n_send // 2
        pieces = pieces + [lax.ppermute(piece, "rep", swap) for piece in pieces]
        places = places + [half + place for place in places]
        block = cols % n_dom
        holder = cols // n_dom
        across = place_of((block // 4) ^ (me % 4), holder)
        other = (holder != rep).astype(jnp.int32)
        slots = ((other * sections + slot[:, None]) * 4 + across) * 4 + block % 4
    else:
        mine = features.at[lines.reshape(-1)].get(mode="promise_in_bounds")
        landed = lax.all_to_all(mine, "dom", 0, 0, tiled=True)
        landed = landed.reshape(n_dom, -1, width)
        shard = landed.at[section_owner].get(mode="promise_in_bounds")
        whole = lax.all_gather(shard, ("rep", "dom"), axis=0)
        whole = whole.transpose(1, 0, 2, 3).reshape(sections * n_send, tile_len, width)
        pieces, places = [whole], [0]
        slots = jnp.arange(sections)[:, None] * n_send + cols
    hidden = products(
        pieces, places, tile_list, rows, slots.reshape(-1), weight, sections * n_send, n_blocks
    )
    return hidden.reshape(n_blocks * tile_len, -1)


def solution(mesh):
    return jax.shard_map(
        body,
        mesh=mesh,
        in_specs=(
            P("dom", None),
            P("dom", None),
            P(),
            P(),
            P("dom", None, "rep"),
            P("dom", None, "rep"),
            P("dom", None, "rep", None, None),
            P(),
        ),
        out_specs=P(("dom", "rep"), None),
        check_vma=False,
    )
```

```python
import functools

import jax
import jax.numpy as jnp
from jax import lax
from jax.experimental import pallas as pl
from jax.experimental.pallas import tpu as pltpu
from jax.sharding import PartitionSpec as P


UNROLL = 8


def load(n_first, pieces, places, sent, sem):
    return [
        pltpu.make_async_copy(piece, sent.at[pl.ds(place, piece.shape[0])], sem.at[n_first + i])
        for i, (piece, place) in enumerate(zip(pieces, places))
    ]


def put(lists, count, here, tile, row, place):
    lists[0, count] = tile
    lists[1, count] = row
    lists[2, count] = place
    return count + here.astype(jnp.int32)


def pad(lists, count, n_blocks):
    for i in range(UNROLL):
        put(lists, count + i, count >= 0, 0, n_blocks, 0)
    return (count + UNROLL - 1) // UNROLL


def run(lists, groups, tiles, sent, acc):
    def step(group, carry):
        at = [group * UNROLL + i for i in range(UNROLL)]
        done = [
            jnp.dot(
                tiles[lists[0, i]], sent[lists[2, i]], preferred_element_type=jnp.float32
            )
            for i in at
        ]
        for i, product in zip(at, done):
            acc[lists[1, i]] += product
        return carry

    lax.fori_loop(0, groups, step, 0)


def finish(acc, weight_ref, out_ref, stage, out_sem):
    steps, group, tile_len = stage.shape[:3]
    copies = []
    for i in range(steps):
        total = acc[pl.ds(i * group, group)].reshape(group * tile_len, acc.shape[2])
        mixed = jnp.dot(
            total.astype(jnp.bfloat16), weight_ref[...], preferred_element_type=jnp.float32
        )
        stage[i] = jnp.maximum(mixed, 0.0).astype(out_ref.dtype).reshape(stage.shape[1:])
        copies.append(
            pltpu.make_async_copy(stage.at[i], out_ref.at[pl.ds(i * group, group)], out_sem.at[i])
        )
        copies[-1].start()
    for copy in copies:
        copy.wait()


def whole_kernel(places, rows_ref, slots_ref, *refs):
    n = len(places)
    tile_ref, weight_ref, out_ref, sent, tiles, acc, stage, lists, sem, out_sem = refs[n:]
    n_tiles, n_blocks = rows_ref.shape[0], out_ref.shape[0]
    copies = load(0, refs[:n], places, sent, sem)
    copies.append(pltpu.make_async_copy(tile_ref, tiles, sem.at[n]))
    for copy in copies:
        copy.start()
    acc[...] = jnp.zeros_like(acc)

    def pick(t, count):
        row = rows_ref[t]
        here = jnp.logical_and(row >= 0, row < n_blocks)
        return put(lists, count, here, t, row, slots_ref[t])

    groups = pad(lists, lax.fori_loop(0, n_tiles, pick, jnp.int32(0)), n_blocks)
    for copy in copies:
        copy.wait()
    run(lists, groups, tiles, sent, acc)
    finish(acc, weight_ref, out_ref, stage, out_sem)


def tile_copies(n_first, tile_refs, section_ref, first_slot, tiles, sem):
    each = tiles.shape[0] // 4
    copies = []
    for i, ref in enumerate(tile_refs):
        for k in range(2):
            at = pl.ds(section_ref[first_slot + k] * each, each)
            copies.append(
                pltpu.make_async_copy(
                    ref.at[at], tiles.at[pl.ds((2 * i + k) * each, each)], sem.at[n_first + 2 * i + k]
                )
            )
    return copies


def first_kernel(places, rows_ref, slots_ref, section_ref, *refs):
    n = len(places)
    pieces, tile_refs = refs[:n], refs[n : n + 2]
    acc_ref, later_ref, sent, tiles, acc, lists, sem = refs[n + 2 :]
    n_blocks = acc_ref.shape[0]
    each = tiles.shape[0] // 4
    copies = load(0, pieces, places, sent, sem)
    copies += tile_copies(n, tile_refs, section_ref, 0, tiles, sem)
    for copy in copies:
        copy.start()
    acc[...] = jnp.zeros_like(acc)
    now, later = jnp.int32(0), jnp.int32(0)
    for part in range(2):
        for slot in range(4):
            first = part * 4 * each + section_ref[slot] * each
            place = (part * 2 + slot % 2) * each

            def pick(k, count):
                row = rows_ref[first + k]
                here = jnp.logical_and(row >= 0, row < n_blocks)
                target = lists if slot < 2 else later_ref
                return put(target, count, here, place + k, row, slots_ref[first + k])

            if slot < 2:
                now = lax.fori_loop(0, each, pick, now)
            else:
                later = lax.fori_loop(0, each, pick, later)
    later_ref[3, 0] = pad(later_ref, later, n_blocks)
    groups = pad(lists, now, n_blocks)
    for copy in copies:
        copy.wait()
    run(lists, groups, tiles, sent, acc)
    save = pltpu.make_async_copy(acc.at[pl.ds(0, n_blocks)], acc_ref, sem.at[0])
    save.start()
    save.wait()


def second_kernel(places, lists, section_ref, *refs):
    n = len(places)
    pieces, tile_refs = refs[:n], refs[n : n + 2]
    acc_ref, weight_ref, out_ref, sent, tiles, acc, stage, sem, out_sem = refs[n + 2 :]
    copies = [pltpu.make_async_copy(acc_ref, acc.at[pl.ds(0, out_ref.shape[0])], sem.at[n + 4])]
    copies += tile_copies(n, tile_refs, section_ref, 2, tiles, sem)
    copies += load(0, pieces, places, sent, sem)
    for copy in copies:
        copy.start()
    for copy in copies:
        copy.wait()
    run(lists, lists[3, 0], tiles, sent, acc)
    finish(acc, weight_ref, out_ref, stage, out_sem)


HBM = pl.BlockSpec(memory_space=pltpu.HBM)
SMEM = pl.BlockSpec(memory_space=pltpu.SMEM)
VMEM = pl.BlockSpec(memory_space=pltpu.VMEM)


def settings(n_products, tile_len, width, n_bytes):
    return {
        "compiler_params": pltpu.CompilerParams(vmem_limit_bytes=60 * 1024 * 1024),
        "cost_estimate": pl.CostEstimate(
            flops=2 * n_products * tile_len * tile_len * width,
            bytes_accessed=n_bytes,
            transcendentals=0,
        ),
    }


def out_stage(n_blocks, tile_len, width):
    group = min(4, n_blocks)
    return pltpu.VMEM((n_blocks // group, group, tile_len, width), jnp.bfloat16)


def products(pieces, places, tiles, rows, slots, weight, n_sent, n_blocks):
    n_tiles, tile_len = tiles.shape[:2]
    width = weight.shape[0]
    return pl.pallas_call(
        functools.partial(whole_kernel, tuple(places)),
        out_shape=jax.ShapeDtypeStruct((n_blocks, tile_len, weight.shape[1]), jnp.bfloat16),
        in_specs=[SMEM, SMEM] + [HBM] * (len(pieces) + 1) + [VMEM],
        out_specs=HBM,
        scratch_shapes=[
            pltpu.VMEM((n_sent, tile_len, width), jnp.bfloat16),
            pltpu.VMEM(tiles.shape, jnp.bfloat16),
            pltpu.VMEM((n_blocks + 1, tile_len, width), jnp.float32),
            out_stage(n_blocks, tile_len, weight.shape[1]),
            pltpu.SMEM((3, n_tiles + UNROLL), jnp.int32),
            pltpu.SemaphoreType.DMA((len(pieces) + 1,)),
            pltpu.SemaphoreType.DMA((n_blocks // min(4, n_blocks),)),
        ],
        **settings(n_tiles, tile_len, width, 16 << 20),
    )(rows, slots, *pieces, tiles, weight)


def products_in_two(pieces, places, tile_list, rows, slots, section_at, weight, n_blocks):
    n_tiles, tile_len = 2 * tile_list[0].shape[0], tile_list[0].shape[1]
    width = weight.shape[0]
    n_sent = 2 * sum(piece.shape[0] for piece in pieces[0][: len(pieces[0]) // 2])
    scratch = [
        pltpu.VMEM((n_sent, tile_len, width), jnp.bfloat16),
        pltpu.VMEM((n_tiles // 2, tile_len, tile_len), jnp.bfloat16),
        pltpu.VMEM((n_blocks + 1, tile_len, width), jnp.float32),
    ]
    lists = (4, n_tiles + UNROLL)
    first, second = pieces
    sums, later = pl.pallas_call(
        functools.partial(first_kernel, tuple(places[0])),
        out_shape=(
            jax.ShapeDtypeStruct((n_blocks, tile_len, width), jnp.float32),
            jax.ShapeDtypeStruct(lists, jnp.int32),
        ),
        in_specs=[SMEM] * 3 + [HBM] * (len(first) + 2),
        out_specs=(HBM, SMEM),
        scratch_shapes=scratch
        + [pltpu.SMEM(lists, jnp.int32), pltpu.SemaphoreType.DMA((len(first) + 4,))],
        **settings(n_tiles // 2, tile_len, width, 10 << 20),
    )(rows, slots, section_at, *first, *tile_list)
    return pl.pallas_call(
        functools.partial(second_kernel, tuple(places[1])),
        out_shape=jax.ShapeDtypeStruct((n_blocks, tile_len, weight.shape[1]), jnp.bfloat16),
        in_specs=[SMEM] * 2 + [HBM] * (len(second) + 3) + [VMEM],
        out_specs=HBM,
        scratch_shapes=scratch
        + [
            out_stage(n_blocks, tile_len, weight.shape[1]),
            pltpu.SemaphoreType.DMA((len(second) + 5,)),
            pltpu.SemaphoreType.DMA((n_blocks // min(4, n_blocks),)),
        ],
        **settings(n_tiles // 2, tile_len, width, 12 << 20),
    )(later, section_at, *second, *tile_list, sums, weight)


def lines_kernel(owner_ref, blocks_ref, order_ref, out_ref):
    me, rep = lax.axis_index("dom"), lax.axis_index("rep")
    sections, n_send = blocks_ref.shape
    section = jnp.int32(0)
    for s in range(sections):
        section = jnp.where(owner_ref[s] == me, s, section)
    each = n_send // 8
    for group, across in enumerate((3, 1 + rep, 2 - rep, 0)):
        base = rep * (n_send // 2) + ((me % 4) ^ across) * each
        for j in range(each):
            block = blocks_ref[section, base + j]
            out_ref[pl.ds(group * each + j, 1), :] = order_ref[pl.ds(block, 1), :]


def share_lines(node_order, section_owner, send_blocks, tile_len):
    return pl.pallas_call(
        lines_kernel,
        out_shape=jax.ShapeDtypeStruct((send_blocks.shape[1] // 2, tile_len), jnp.int32),
        in_specs=[SMEM, SMEM, VMEM],
        out_specs=VMEM,
    )(section_owner, send_blocks, node_order[0].reshape(-1, tile_len))


def share_rows(node_order, section_owner, send_blocks, tile_len):
    me = lax.axis_index("dom")
    sections, n_send = send_blocks.shape
    mine = (section_owner == me).astype(jnp.int32)
    section = jnp.sum(mine * jnp.arange(sections, dtype=jnp.int32))
    share = n_send // lax.axis_size("rep")
    picks = lax.dynamic_slice(
        send_blocks, (section, lax.axis_index("rep") * share), (1, share)
    )[0]
    order = node_order[0].reshape(-1, tile_len)
    return order.at[picks].get(mode="promise_in_bounds")


def move(value, pairs):
    return lax.ppermute(value, "dom", pairs)


def flip(bits):
    return [(i, i ^ bits) for i in range(16)]


def cross(value, turn):
    pairs = []
    for i in range(16):
        for core in (0, 1):
            pairs.append((2 * i + core, 2 * (i ^ (1 if core == turn else 2)) + core))
    return lax.ppermute(value, ("dom", "rep"), pairs)


def place_of(across, core):
    return jnp.where(core == 0, across, (across & 1) * 2 + across // 2)


def quad_scatter(features, lines):
    each = lines.shape[0] // 4

    def rows(first):
        taken = features.at[lines[first : first + 2 * each].reshape(-1)].get(
            mode="promise_in_bounds"
        )
        return taken.reshape(2 * each, lines.shape[1], features.shape[1])

    by_first = cross(rows(0), 0)
    kept = rows(2 * each)
    by_second = cross(jnp.concatenate([kept[:each], by_first[:each]]), 1)
    return kept[each:], by_first[each:], by_second[:each], by_second[each:]


INWARD = [(i, i + 4) for i in range(4)] + [(i, i - 4) for i in range(12, 16)]
MIDDLE = [(i, i + 4) for i in range(4, 8)] + [(i, i - 4) for i in range(8, 12)]
OUTWARD = [(i, i - 4) for i in range(4, 8)] + [(i, i + 4) for i in range(8, 12)]


def tie(value, after):
    return lax.optimization_barrier((value, after))[0]


def along_z(first, at, z, near):
    inner = jnp.logical_or(z == 1, z == 2)
    own = at == z
    known = jnp.where(own, first, near)
    across = move(known, MIDDLE)
    beyond = move(jnp.where(own, first, across), OUTWARD)
    same_half = (at // 2) == (z // 2)
    return jnp.where(inner, jnp.where(same_half, known, across), jnp.where(own, first, beyond))


def along_z_ends(first, z):
    outer = jnp.logical_or(z == 0, z == 3)
    came = move(first, INWARD)
    near = jnp.where(outer, first, came)
    across = move(came, MIDDLE)
    beyond = move(across, OUTWARD)
    return came, near, jnp.where(outer, beyond, across)


def quad_gather(own, after):
    came = cross(own if after is None else tie(own, after), 0)
    pair = jnp.concatenate([own, came])
    return came, [pair, cross(pair, 1)]


def gather_small(features, lines, section_owner):
    me = lax.axis_index("dom")
    quad, z = me % 4, me // 4
    held = quad_scatter(features, lines)
    is_first, is_last = section_owner == 0, section_owner == 15
    other = jnp.logical_not(jnp.logical_or(is_first, is_last))
    rank = jnp.cumsum(other.astype(jnp.int32)) - 1
    owners = [
        jnp.sum(jnp.where(jnp.logical_and(other, rank == i), section_owner, 0)) for i in (0, 1)
    ]
    low = z < 2
    slot = jnp.where(other, 2 + rank, jnp.where(is_first == low, 0, 1))

    def of(source):
        return lax.select_n(place_of(quad ^ source, lax.axis_index("rep")), *held)

    came, near, far = along_z_ends(of(jnp.where(low, 0, 3)), z)
    quarters = [near, far]
    for owner in owners:
        first = of(owner % 4)
        came = move(tie(first, came), INWARD)
        quarters.append(along_z(first, owner // 4, z, came))
    pieces, after = [], None
    for quarter in quarters:
        after, made = quad_gather(quarter, after)
        pieces += made
    return pieces, slot


def body(features, node_order, section_owner, send_blocks, tile_rows, tile_cols, tiles, weight):
    width = features.shape[1]
    tile_len = tiles.shape[3]
    blocks = features.shape[0] // tile_len
    n_dom, n_rep = lax.axis_size("dom"), lax.axis_size("rep")
    sections, n_send = send_blocks.shape
    me, rep = lax.axis_index("dom"), lax.axis_index("rep")
    n_blocks = blocks // n_rep
    small = n_dom == 16 and n_rep == 2 and n_send == n_dom * n_rep

    own_tiles = tiles[0].reshape(-1, tile_len, tile_len)
    numbers = jnp.stack([tile_rows[0], tile_cols[0]])
    if small:
        swap = [(0, 1), (1, 0)]

        def exchange(value):
            return lax.ppermute(value, "rep", swap)

        tile_list = [own_tiles, exchange(own_tiles)]
        numbers = jnp.stack([numbers, exchange(numbers)])
        rows = (numbers[:, 0] - rep * n_blocks).reshape(-1)
        cols = numbers[:, 1]
        lines = share_lines(node_order, section_owner, send_blocks, tile_len)
        pieces, slot = gather_small(features, lines, section_owner)
        quarter = n_dom // 4
        holder, block = cols // n_dom, cols % n_dom
        at = place_of((block // quarter) ^ (me % 4), holder) * quarter + block % quarter
        slots = ((holder != rep) * 2 + slot[:, None] % 2) * n_dom + at
        section_at = jnp.sum(
            jnp.where(slot[None, :] == jnp.arange(4)[:, None], jnp.arange(sections), 0), axis=1
        ).astype(jnp.int32)
        parts, places = [], []
        for first in (0, 4):
            own = pieces[first : first + 4]
            parts.append(own + [exchange(piece) for piece in own])
            places.append([i * 2 * quarter for i in range(8)])
        hidden = products_in_two(
            parts, places, tile_list, rows, slots.reshape(-1), section_at, weight, n_blocks
        )
    else:
        tile_list = lax.all_gather(own_tiles, "rep", axis=0, tiled=True)
        numbers = lax.all_gather(numbers, "rep", axis=0)
        rows = (numbers[:, 0] - rep * n_blocks).reshape(-1)
        lines = share_rows(node_order, section_owner, send_blocks, tile_len)
        mine = features.at[lines.reshape(-1)].get(mode="promise_in_bounds")
        landed = lax.all_to_all(mine, "dom", 0, 0, tiled=True)
        landed = landed.reshape(n_dom, -1, width)
        shard = landed.at[section_owner].get(mode="promise_in_bounds")
        whole = lax.all_gather(shard, ("rep", "dom"), axis=0)
        whole = whole.transpose(1, 0, 2, 3).reshape(sections * n_send, tile_len, width)
        slots = jnp.arange(sections)[:, None] * n_send + numbers[:, 1]
        hidden = products(
            [whole], [0], tile_list, rows, slots.reshape(-1), weight, sections * n_send, n_blocks
        )
    return hidden.reshape(n_blocks * tile_len, -1)


def solution(mesh):
    return jax.shard_map(
        body,
        mesh=mesh,
        in_specs=(
            P("dom", None),
            P("dom", None),
            P(),
            P(),
            P("dom", None, "rep"),
            P("dom", None, "rep"),
            P("dom", None, "rep", None, None),
            P(),
        ),
        out_specs=P(("dom", "rep"), None),
        check_vma=False,
    )
```

```python
import functools

import jax
import jax.numpy as jnp
from jax import lax
from jax.experimental import pallas as pl
from jax.experimental.pallas import tpu as pltpu
from jax.sharding import PartitionSpec as P


UNROLL = 8


def load(n_first, pieces, places, sent, sem):
    return [
        pltpu.make_async_copy(piece, sent.at[pl.ds(place, piece.shape[0])], sem.at[n_first + i])
        for i, (piece, place) in enumerate(zip(pieces, places))
    ]


def put(lists, count, here, tile, row, place):
    lists[0, count] = tile
    lists[1, count] = row
    lists[2, count] = place
    return count + here.astype(jnp.int32)


def pad(lists, first, count, n_blocks):
    for i in range(UNROLL):
        put(lists, first + count + i, count >= 0, 0, n_blocks, 0)
    return (count + UNROLL - 1) // UNROLL


def run(lists, first, groups, tiles, sent, acc):
    def step(group, carry):
        at = [first + group * UNROLL + i for i in range(UNROLL)]
        done = [
            jnp.dot(
                tiles[lists[0, i]], sent[lists[2, i]], preferred_element_type=jnp.float32
            )
            for i in at
        ]
        for i, product in zip(at, done):
            acc[lists[1, i]] += product
        return carry

    lax.fori_loop(0, groups, step, 0)


def finish(acc, weight_ref, out_ref, stage, out_sem):
    steps, group, tile_len = stage.shape[:3]
    copies = []
    for i in range(steps):
        total = acc[pl.ds(i * group, group)].reshape(group * tile_len, acc.shape[2])
        mixed = jnp.dot(
            total.astype(jnp.bfloat16), weight_ref[...], preferred_element_type=jnp.float32
        )
        stage[i] = jnp.maximum(mixed, 0.0).astype(out_ref.dtype).reshape(stage.shape[1:])
        copies.append(
            pltpu.make_async_copy(stage.at[i], out_ref.at[pl.ds(i * group, group)], out_sem.at[i])
        )
        copies[-1].start()
    for copy in copies:
        copy.wait()


def whole_kernel(places, rows_ref, slots_ref, *refs):
    n = len(places)
    tile_ref, weight_ref, out_ref, sent, tiles, acc, stage, lists, sem, out_sem = refs[n:]
    n_tiles, n_blocks = rows_ref.shape[0], out_ref.shape[0]
    copies = load(0, refs[:n], places, sent, sem)
    copies.append(pltpu.make_async_copy(tile_ref, tiles, sem.at[n]))
    for copy in copies:
        copy.start()
    acc[...] = jnp.zeros_like(acc)

    def pick(t, count):
        row = rows_ref[t]
        here = jnp.logical_and(row >= 0, row < n_blocks)
        return put(lists, count, here, t, row, slots_ref[t])

    groups = pad(lists, 0, lax.fori_loop(0, n_tiles, pick, jnp.int32(0)), n_blocks)
    for copy in copies:
        copy.wait()
    run(lists, 0, groups, tiles, sent, acc)
    finish(acc, weight_ref, out_ref, stage, out_sem)


def phased_kernel(places, lists, *refs):
    counts = [len(part) for part in places]
    n = sum(counts)
    pieces, tile_refs = refs[:n], refs[n : n + 2]
    weight_ref, out_ref, sent, tiles, acc, stage, sem, out_sem = refs[n + 2 :]
    each = tiles.shape[0] // 2
    copies = [
        pltpu.make_async_copy(ref, tiles.at[pl.ds(i * each, each)], sem.at[n + i])
        for i, ref in enumerate(tile_refs)
    ]
    copies += load(0, pieces[: counts[0]], places[0], sent, sem)
    later = load(counts[0], pieces[counts[0] :], places[1], sent, sem)
    for copy in copies + later:
        copy.start()
    acc[...] = jnp.zeros_like(acc)
    middle = lists.shape[1] // 2
    for copy in copies:
        copy.wait()
    run(lists, 0, lists[3, 0], tiles, sent, acc)
    for copy in later:
        copy.wait()
    run(lists, middle, lists[3, middle], tiles, sent, acc)
    finish(acc, weight_ref, out_ref, stage, out_sem)


def lists_kernel(n_blocks, owner_ref, own_ref, other_ref, lists):
    me, rep = lax.axis_index("dom"), lax.axis_index("rep")
    quad, z = me % 4, me // 4
    sections, each = own_ref.shape[1:]
    middle = lists.shape[1] // 2
    known, others, rank = jnp.int32(0), jnp.int32(0), jnp.int32(0)
    for s in range(sections):
        owner = owner_ref[s]
        is_end = jnp.logical_or(owner == 0, owner == 15)
        slot = jnp.where(is_end, ((owner == 0) != (z < 2)).astype(jnp.int32), rank)
        rank = rank + 1 - is_end.astype(jnp.int32)
        for part, ref in enumerate((own_ref, other_ref)):

            def pick(k, counts, ref=ref, part=part, s=s, slot=slot, owner=owner, is_end=is_end):
                row = ref[0, s, k] - rep * n_blocks
                here = jnp.logical_and(row >= 0, row < n_blocks)
                col = ref[1, s, k]
                holder, quarter, within = col // 16, (col % 16) // 4, col % 4
                base = jnp.where(holder == rep, 0, 32)
                at_end = place_of(quarter ^ quad, holder) + 4 * slot
                turn = place_of(quarter ^ (owner % 4), holder)
                chip = jnp.where(turn == 0, 3, jnp.where(turn == 3, 0, turn)) * 4 + within
                shift = (chip // 4 - z) & 3
                by = place_of((chip % 4) ^ quad, holder)
                at_other = jnp.where(
                    (shift & 1) == 1,
                    8 + by * 4 + (shift // 2) * 2,
                    jnp.where(shift == 0, 0, 24) + by * 2,
                )
                place = jnp.where(is_end, base + at_end * 4 + within, 64 + base + at_other + slot)
                tile = (part * sections + s) * each + k
                known, others = counts
                target = jnp.where(is_end, known, middle + others)
                put(lists, target, here, tile, row, place)
                now = here.astype(jnp.int32)
                return known + jnp.where(is_end, now, 0), others + jnp.where(is_end, 0, now)

            known, others = lax.fori_loop(0, each, pick, (known, others))
    lists[3, 0] = pad(lists, 0, known, n_blocks)
    lists[3, middle] = pad(lists, middle, others, n_blocks)


HBM = pl.BlockSpec(memory_space=pltpu.HBM)
SMEM = pl.BlockSpec(memory_space=pltpu.SMEM)
VMEM = pl.BlockSpec(memory_space=pltpu.VMEM)


def settings(n_products, tile_len, width, n_bytes):
    return {
        "compiler_params": pltpu.CompilerParams(vmem_limit_bytes=60 * 1024 * 1024),
        "cost_estimate": pl.CostEstimate(
            flops=2 * n_products * tile_len * tile_len * width,
            bytes_accessed=n_bytes,
            transcendentals=0,
        ),
    }


def out_stage(n_blocks, tile_len, width):
    group = min(4, n_blocks)
    return pltpu.VMEM((n_blocks // group, group, tile_len, width), jnp.bfloat16)


def products(pieces, places, tiles, rows, slots, weight, n_sent, n_blocks):
    n_tiles, tile_len = tiles.shape[:2]
    width = weight.shape[0]
    return pl.pallas_call(
        functools.partial(whole_kernel, tuple(places)),
        out_shape=jax.ShapeDtypeStruct((n_blocks, tile_len, weight.shape[1]), jnp.bfloat16),
        in_specs=[SMEM, SMEM] + [HBM] * (len(pieces) + 1) + [VMEM],
        out_specs=HBM,
        scratch_shapes=[
            pltpu.VMEM((n_sent, tile_len, width), jnp.bfloat16),
            pltpu.VMEM(tiles.shape, jnp.bfloat16),
            pltpu.VMEM((n_blocks + 1, tile_len, width), jnp.float32),
            out_stage(n_blocks, tile_len, weight.shape[1]),
            pltpu.SMEM((3, n_tiles + UNROLL), jnp.int32),
            pltpu.SemaphoreType.DMA((len(pieces) + 1,)),
            pltpu.SemaphoreType.DMA((n_blocks // min(4, n_blocks),)),
        ],
        **settings(n_tiles, tile_len, width, 16 << 20),
    )(rows, slots, *pieces, tiles, weight)


def products_in_phases(pieces, places, tile_list, lists, weight, n_blocks):
    n_tiles, tile_len = 2 * tile_list[0].shape[0], tile_list[0].shape[1]
    width = weight.shape[0]
    flat = pieces[0] + pieces[1]
    n_sent = sum(piece.shape[0] for piece in flat)
    return pl.pallas_call(
        functools.partial(phased_kernel, places),
        out_shape=jax.ShapeDtypeStruct((n_blocks, tile_len, weight.shape[1]), jnp.bfloat16),
        in_specs=[SMEM] + [HBM] * (len(flat) + 2) + [VMEM],
        out_specs=HBM,
        scratch_shapes=[
            pltpu.VMEM((n_sent, tile_len, width), jnp.bfloat16),
            pltpu.VMEM((n_tiles, tile_len, tile_len), jnp.bfloat16),
            pltpu.VMEM((n_blocks + 1, tile_len, width), jnp.float32),
            out_stage(n_blocks, tile_len, weight.shape[1]),
            pltpu.SemaphoreType.DMA((len(flat) + 2,)),
            pltpu.SemaphoreType.DMA((n_blocks // min(4, n_blocks),)),
        ],
        **settings(n_tiles, tile_len, width, 16 << 20),
    )(lists, *flat, *tile_list, weight)


def product_lists(section_owner, own, other, n_blocks):
    n_tiles = 2 * own.shape[1] * own.shape[2]
    return pl.pallas_call(
        functools.partial(lists_kernel, n_blocks),
        out_shape=jax.ShapeDtypeStruct((4, 2 * (n_tiles + UNROLL)), jnp.int32),
        in_specs=[SMEM] * 3,
        out_specs=SMEM,
    )(section_owner, own, other)


def lines_kernel(owner_ref, blocks_ref, order_ref, out_ref):
    me, rep = lax.axis_index("dom"), lax.axis_index("rep")
    sections, n_send = blocks_ref.shape
    section = jnp.int32(0)
    for s in range(sections):
        section = jnp.where(owner_ref[s] == me, s, section)
    each = n_send // 8
    for group, across in enumerate((3, 1 + rep, 2 - rep, 0)):
        base = rep * (n_send // 2) + ((me % 4) ^ across) * each
        for j in range(each):
            block = blocks_ref[section, base + j]
            out_ref[pl.ds(group * each + j, 1), :] = order_ref[pl.ds(block, 1), :]


def share_lines(node_order, section_owner, send_blocks, tile_len):
    return pl.pallas_call(
        lines_kernel,
        out_shape=jax.ShapeDtypeStruct((send_blocks.shape[1] // 2, tile_len), jnp.int32),
        in_specs=[SMEM, SMEM, VMEM],
        out_specs=VMEM,
    )(section_owner, send_blocks, node_order[0].reshape(-1, tile_len))


def share_rows(node_order, section_owner, send_blocks, tile_len):
    me = lax.axis_index("dom")
    sections, n_send = send_blocks.shape
    mine = (section_owner == me).astype(jnp.int32)
    section = jnp.sum(mine * jnp.arange(sections, dtype=jnp.int32))
    share = n_send // lax.axis_size("rep")
    picks = lax.dynamic_slice(
        send_blocks, (section, lax.axis_index("rep") * share), (1, share)
    )[0]
    order = node_order[0].reshape(-1, tile_len)
    return order.at[picks].get(mode="promise_in_bounds")


def move(value, pairs):
    return lax.ppermute(value, "dom", pairs)


def flip(bits):
    return [(i, i ^ bits) for i in range(16)]


def cross(value, turn):
    pairs = []
    for i in range(16):
        for core in (0, 1):
            pairs.append((2 * i + core, 2 * (i ^ (1 if core == turn else 2)) + core))
    return lax.ppermute(value, ("dom", "rep"), pairs)


def place_of(across, core):
    return jnp.where(core == 0, across, (across & 1) * 2 + across // 2)


def quad_scatter(rows):
    each = rows.shape[0] // 4
    by_first = cross(rows[: 2 * each], 0)
    by_second = cross(jnp.concatenate([rows[2 * each : 3 * each], by_first[:each]]), 1)
    return rows[3 * each :], by_first[each:], by_second[:each], by_second[each:]


INWARD = [(i, i + 4) for i in range(4)] + [(i, i - 4) for i in range(12, 16)]
MIDDLE = [(i, i + 4) for i in range(4, 8)] + [(i, i - 4) for i in range(8, 12)]
OUTWARD = [(i, i - 4) for i in range(4, 8)] + [(i, i + 4) for i in range(8, 12)]


def tie(value, after):
    return lax.optimization_barrier((value, after))[0]


def along_z_ends(first, z):
    outer = jnp.logical_or(z == 0, z == 3)
    came = move(first, INWARD)
    near = jnp.where(outer, first, came)
    across = move(came, MIDDLE)
    beyond = move(across, OUTWARD)
    return came, near, jnp.where(outer, beyond, across)


def quad_gather(own):
    pair = jnp.concatenate([own, cross(own, 0)])
    return [pair, cross(pair, 1)]


RING = {
    k: [(z * 4 + q, ((z - k) % 4) * 4 + q) for z in range(4) for q in range(4)] for k in (1, 2, 3)
}


def gather_ends(rows):
    me = lax.axis_index("dom")
    quad, z = me % 4, me // 4
    held = quad_scatter(rows)
    source = jnp.where(z < 2, 0, 3)
    quarter = lax.select_n(place_of(quad ^ source, lax.axis_index("rep")), *held)
    came, near, far = along_z_ends(quarter, z)
    return quad_gather(near) + quad_gather(far)


def gather_others(rows, section_owner):
    is_end = jnp.logical_or(section_owner == 0, section_owner == 15)
    rank = jnp.cumsum(1 - is_end.astype(jnp.int32)) - 1
    owners = jnp.stack(
        [jnp.sum(jnp.where(jnp.logical_or(is_end, rank != i), 0, section_owner)) for i in (0, 1)]
    )
    landed = lax.all_to_all(rows, "dom", 0, 0, tiled=True)
    shard = landed.at[owners].get(mode="promise_in_bounds")
    near = [move(shard, RING[1]), move(shard, RING[3])]
    far = move(tie(shard, near[0]), RING[2])
    return quad_gather(shard) + quad_gather(jnp.concatenate(near)) + quad_gather(far)


def body(features, node_order, section_owner, send_blocks, tile_rows, tile_cols, tiles, weight):
    width = features.shape[1]
    tile_len = tiles.shape[3]
    blocks = features.shape[0] // tile_len
    n_dom, n_rep = lax.axis_size("dom"), lax.axis_size("rep")
    sections, n_send = send_blocks.shape
    me, rep = lax.axis_index("dom"), lax.axis_index("rep")
    n_blocks = blocks // n_rep
    small = n_dom == 16 and n_rep == 2 and n_send == n_dom * n_rep

    own_tiles = tiles[0].reshape(-1, tile_len, tile_len)
    numbers = jnp.stack([tile_rows[0], tile_cols[0]])
    if small:
        swap = [(0, 1), (1, 0)]

        def exchange(value):
            return lax.ppermute(value, "rep", swap)

        tile_list = [own_tiles, exchange(own_tiles)]
        lists = product_lists(section_owner, numbers, exchange(numbers), n_blocks)
        lines = share_lines(node_order, section_owner, send_blocks, tile_len)
        mine = features.at[lines.reshape(-1)].get(mode="promise_in_bounds")
        mine = mine.reshape(-1, tile_len, width)
        own = [gather_ends(mine), gather_others(mine, section_owner)]
        parts = [part + [exchange(piece) for piece in part] for part in own]
        ends, place = [], 0
        for part in parts:
            ends.append([])
            for piece in part:
                ends[-1].append(place)
                place += piece.shape[0]
        hidden = products_in_phases(parts, ends, tile_list, lists, weight, n_blocks)
    else:
        tile_list = lax.all_gather(own_tiles, "rep", axis=0, tiled=True)
        numbers = lax.all_gather(numbers, "rep", axis=0)
        rows = (numbers[:, 0] - rep * n_blocks).reshape(-1)
        lines = share_rows(node_order, section_owner, send_blocks, tile_len)
        mine = features.at[lines.reshape(-1)].get(mode="promise_in_bounds")
        landed = lax.all_to_all(mine, "dom", 0, 0, tiled=True)
        landed = landed.reshape(n_dom, -1, width)
        shard = landed.at[section_owner].get(mode="promise_in_bounds")
        whole = lax.all_gather(shard, ("rep", "dom"), axis=0)
        whole = whole.transpose(1, 0, 2, 3).reshape(sections * n_send, tile_len, width)
        slots = jnp.arange(sections)[:, None] * n_send + numbers[:, 1]
        hidden = products(
            [whole], [0], tile_list, rows, slots.reshape(-1), weight, sections * n_send, n_blocks
        )
    return hidden.reshape(n_blocks * tile_len, -1)


def solution(mesh):
    return jax.shard_map(
        body,
        mesh=mesh,
        in_specs=(
            P("dom", None),
            P("dom", None),
            P(),
            P(),
            P("dom", None, "rep"),
            P("dom", None, "rep"),
            P("dom", None, "rep", None, None),
            P(),
        ),
        out_specs=P(("dom", "rep"), None),
        check_vma=False,
    )
```

```python
import functools

import jax
import jax.numpy as jnp
from jax import lax
from jax.experimental import pallas as pl
from jax.experimental.pallas import tpu as pltpu
from jax.sharding import PartitionSpec as P


UNROLL = 8


def load(n_first, pieces, places, sent, sem):
    return [
        pltpu.make_async_copy(piece, sent.at[pl.ds(place, piece.shape[0])], sem.at[n_first + i])
        for i, (piece, place) in enumerate(zip(pieces, places))
    ]


def put(lists, count, here, tile, row, place):
    lists[0, count] = tile
    lists[1, count] = row
    lists[2, count] = place
    return count + here.astype(jnp.int32)


def pad(lists, first, count, n_blocks):
    for i in range(UNROLL):
        put(lists, first + count + i, count >= 0, 0, n_blocks, 0)
    return (count + UNROLL - 1) // UNROLL


def run(lists, first, groups, tiles, sent, acc):
    def step(group, carry):
        at = [first + group * UNROLL + i for i in range(UNROLL)]
        done = [
            jnp.dot(
                tiles[lists[0, i]], sent[lists[2, i]], preferred_element_type=jnp.float32
            )
            for i in at
        ]
        for i, product in zip(at, done):
            acc[lists[1, i]] += product
        return carry

    lax.fori_loop(0, groups, step, 0)


def finish(acc, weight_ref, out_ref, stage, out_sem):
    steps, group, tile_len = stage.shape[:3]
    copies = []
    for i in range(steps):
        total = acc[pl.ds(i * group, group)].reshape(group * tile_len, acc.shape[2])
        mixed = jnp.dot(
            total.astype(jnp.bfloat16), weight_ref[...], preferred_element_type=jnp.float32
        )
        stage[i] = jnp.maximum(mixed, 0.0).astype(out_ref.dtype).reshape(stage.shape[1:])
        copies.append(
            pltpu.make_async_copy(stage.at[i], out_ref.at[pl.ds(i * group, group)], out_sem.at[i])
        )
        copies[-1].start()
    for copy in copies:
        copy.wait()


def whole_kernel(places, rows_ref, slots_ref, *refs):
    n = len(places)
    tile_ref, weight_ref, out_ref, sent, tiles, acc, stage, lists, sem, out_sem = refs[n:]
    n_tiles, n_blocks = rows_ref.shape[0], out_ref.shape[0]
    copies = load(0, refs[:n], places, sent, sem)
    copies.append(pltpu.make_async_copy(tile_ref, tiles, sem.at[n]))
    for copy in copies:
        copy.start()
    acc[...] = jnp.zeros_like(acc)

    def pick(t, count):
        row = rows_ref[t]
        here = jnp.logical_and(row >= 0, row < n_blocks)
        return put(lists, count, here, t, row, slots_ref[t])

    groups = pad(lists, 0, lax.fori_loop(0, n_tiles, pick, jnp.int32(0)), n_blocks)
    for copy in copies:
        copy.wait()
    run(lists, 0, groups, tiles, sent, acc)
    finish(acc, weight_ref, out_ref, stage, out_sem)


def phased_kernel(places, lists, *refs):
    counts = [len(part) for part in places]
    n = sum(counts)
    pieces, tile_refs = refs[:n], refs[n : n + 2]
    weight_ref, out_ref, sent, tiles, acc, stage, sem, out_sem = refs[n + 2 :]
    each = tiles.shape[0] // 2
    copies = [
        pltpu.make_async_copy(ref, tiles.at[pl.ds(i * each, each)], sem.at[n + i])
        for i, ref in enumerate(tile_refs)
    ]
    copies += load(0, pieces[: counts[0]], places[0], sent, sem)
    later = load(counts[0], pieces[counts[0] :], places[1], sent, sem)
    for copy in copies + later:
        copy.start()
    acc[...] = jnp.zeros_like(acc)
    middle = lists.shape[1] // 2
    for copy in copies:
        copy.wait()
    run(lists, 0, lists[3, 0], tiles, sent, acc)
    for copy in later:
        copy.wait()
    run(lists, middle, lists[3, middle], tiles, sent, acc)
    finish(acc, weight_ref, out_ref, stage, out_sem)


def lists_kernel(n_blocks, own_ref, other_ref, lists):
    me, rep = lax.axis_index("dom"), lax.axis_index("rep")
    sections, each = own_ref.shape[1:]
    middle = lists.shape[1] // 2
    early, late = jnp.int32(0), jnp.int32(0)
    for s in range(sections):
        for part, ref in enumerate((own_ref, other_ref)):

            def pick(k, counts, ref=ref, part=part, s=s):
                early, late = counts
                row = ref[0, s, k] - rep * n_blocks
                here = jnp.logical_and(row >= 0, row < n_blocks)
                col = ref[1, s, k]
                holder, chip = col // 16, col % 16
                other = (holder != rep).astype(jnp.int32)
                shift = (chip // 4 - me // 4) & 3
                at = place_of((chip ^ me) & 3, holder) * sections + s
                at = jnp.where((shift & 1) == 1, 4 * sections + at + (at // 4 + shift // 2) * 4, at)
                is_late = shift == 2
                place = jnp.where(is_late, 96 + other * 16 + at, other * 48 + at)
                put(
                    lists,
                    jnp.where(is_late, middle + late, early),
                    here,
                    (part * sections + s) * each + k,
                    row,
                    place,
                )
                now = here.astype(jnp.int32)
                return early + jnp.where(is_late, 0, now), late + jnp.where(is_late, now, 0)

            early, late = lax.fori_loop(0, each, pick, (early, late))
    lists[3, 0] = pad(lists, 0, early, n_blocks)
    lists[3, middle] = pad(lists, middle, late, n_blocks)


HBM = pl.BlockSpec(memory_space=pltpu.HBM)
SMEM = pl.BlockSpec(memory_space=pltpu.SMEM)
VMEM = pl.BlockSpec(memory_space=pltpu.VMEM)


def settings(n_products, tile_len, width, n_bytes):
    return {
        "compiler_params": pltpu.CompilerParams(vmem_limit_bytes=60 * 1024 * 1024),
        "cost_estimate": pl.CostEstimate(
            flops=2 * n_products * tile_len * tile_len * width,
            bytes_accessed=n_bytes,
            transcendentals=0,
        ),
    }


def out_stage(n_blocks, tile_len, width):
    group = min(4, n_blocks)
    return pltpu.VMEM((n_blocks // group, group, tile_len, width), jnp.bfloat16)


def products(pieces, places, tiles, rows, slots, weight, n_sent, n_blocks):
    n_tiles, tile_len = tiles.shape[:2]
    width = weight.shape[0]
    return pl.pallas_call(
        functools.partial(whole_kernel, tuple(places)),
        out_shape=jax.ShapeDtypeStruct((n_blocks, tile_len, weight.shape[1]), jnp.bfloat16),
        in_specs=[SMEM, SMEM] + [HBM] * (len(pieces) + 1) + [VMEM],
        out_specs=HBM,
        scratch_shapes=[
            pltpu.VMEM((n_sent, tile_len, width), jnp.bfloat16),
            pltpu.VMEM(tiles.shape, jnp.bfloat16),
            pltpu.VMEM((n_blocks + 1, tile_len, width), jnp.float32),
            out_stage(n_blocks, tile_len, weight.shape[1]),
            pltpu.SMEM((3, n_tiles + UNROLL), jnp.int32),
            pltpu.SemaphoreType.DMA((len(pieces) + 1,)),
            pltpu.SemaphoreType.DMA((n_blocks // min(4, n_blocks),)),
        ],
        **settings(n_tiles, tile_len, width, 16 << 20),
    )(rows, slots, *pieces, tiles, weight)


def products_in_phases(pieces, places, tile_list, lists, weight, n_blocks):
    n_tiles, tile_len = 2 * tile_list[0].shape[0], tile_list[0].shape[1]
    width = weight.shape[0]
    flat = pieces[0] + pieces[1]
    n_sent = sum(piece.shape[0] for piece in flat)
    return pl.pallas_call(
        functools.partial(phased_kernel, places),
        out_shape=jax.ShapeDtypeStruct((n_blocks, tile_len, weight.shape[1]), jnp.bfloat16),
        in_specs=[SMEM] + [HBM] * (len(flat) + 2) + [VMEM],
        out_specs=HBM,
        scratch_shapes=[
            pltpu.VMEM((n_sent, tile_len, width), jnp.bfloat16),
            pltpu.VMEM((n_tiles, tile_len, tile_len), jnp.bfloat16),
            pltpu.VMEM((n_blocks + 1, tile_len, width), jnp.float32),
            out_stage(n_blocks, tile_len, weight.shape[1]),
            pltpu.SemaphoreType.DMA((len(flat) + 2,)),
            pltpu.SemaphoreType.DMA((n_blocks // min(4, n_blocks),)),
        ],
        **settings(n_tiles, tile_len, width, 16 << 20),
    )(lists, *flat, *tile_list, weight)


def product_lists(own, other, n_blocks):
    n_tiles = 2 * own.shape[1] * own.shape[2]
    return pl.pallas_call(
        functools.partial(lists_kernel, n_blocks),
        out_shape=jax.ShapeDtypeStruct((4, 2 * (n_tiles + UNROLL)), jnp.int32),
        in_specs=[SMEM] * 2,
        out_specs=SMEM,
    )(own, other)


def lines_kernel(owner_ref, blocks_ref, order_ref, out_ref):
    me, rep = lax.axis_index("dom"), lax.axis_index("rep")
    sections = blocks_ref.shape[0]
    section = jnp.int32(0)
    for s in range(sections):
        section = jnp.where(owner_ref[s] == me, s, section)
    share = out_ref.shape[0]
    for j in range(share):
        block = blocks_ref[section, rep * share + j]
        out_ref[pl.ds(j, 1), :] = order_ref[pl.ds(block, 1), :]


def share_lines(node_order, section_owner, send_blocks, tile_len):
    return pl.pallas_call(
        lines_kernel,
        out_shape=jax.ShapeDtypeStruct((send_blocks.shape[1] // 2, tile_len), jnp.int32),
        in_specs=[SMEM, SMEM, VMEM],
        out_specs=VMEM,
    )(section_owner, send_blocks, node_order[0].reshape(-1, tile_len))


def share_rows(node_order, section_owner, send_blocks, tile_len):
    me = lax.axis_index("dom")
    sections, n_send = send_blocks.shape
    mine = (section_owner == me).astype(jnp.int32)
    section = jnp.sum(mine * jnp.arange(sections, dtype=jnp.int32))
    share = n_send // lax.axis_size("rep")
    picks = lax.dynamic_slice(
        send_blocks, (section, lax.axis_index("rep") * share), (1, share)
    )[0]
    order = node_order[0].reshape(-1, tile_len)
    return order.at[picks].get(mode="promise_in_bounds")


def move(value, pairs):
    return lax.ppermute(value, "dom", pairs)


def flip(bits):
    return [(i, i ^ bits) for i in range(16)]


def cross(value, turn):
    pairs = []
    for i in range(16):
        for core in (0, 1):
            pairs.append((2 * i + core, 2 * (i ^ (1 if core == turn else 2)) + core))
    return lax.ppermute(value, ("dom", "rep"), pairs)


def place_of(across, core):
    return jnp.where(core == 0, across, (across & 1) * 2 + across // 2)


def tie(value, after):
    return lax.optimization_barrier((value, after))[0]


def quad_gather(own):
    pair = jnp.concatenate([own, cross(own, 0)])
    return [pair, cross(pair, 1)]


RING = {
    k: [(z * 4 + q, ((z - k) % 4) * 4 + q) for z in range(4) for q in range(4)] for k in (1, 2, 3)
}


def gather_small(rows, section_owner, lists):
    landed = lax.all_to_all(rows, "dom", 0, 0, tiled=True)
    shard = landed.at[section_owner].get(mode="promise_in_bounds")
    shard, lists = lax.optimization_barrier((shard, lists))
    near = [move(shard, RING[1]), move(shard, RING[3])]
    far = move(tie(shard, near[0]), RING[2])
    early = quad_gather(shard) + quad_gather(jnp.concatenate(near))
    return early, quad_gather(far), lists


def body(features, node_order, section_owner, send_blocks, tile_rows, tile_cols, tiles, weight):
    width = features.shape[1]
    tile_len = tiles.shape[3]
    blocks = features.shape[0] // tile_len
    n_dom, n_rep = lax.axis_size("dom"), lax.axis_size("rep")
    sections, n_send = send_blocks.shape
    me, rep = lax.axis_index("dom"), lax.axis_index("rep")
    n_blocks = blocks // n_rep
    small = n_dom == 16 and n_rep == 2 and n_send == n_dom * n_rep

    own_tiles = tiles[0].reshape(-1, tile_len, tile_len)
    numbers = jnp.stack([tile_rows[0], tile_cols[0]])
    if small:
        swap = [(0, 1), (1, 0)]

        def exchange(value):
            return lax.ppermute(value, "rep", swap)

        tile_list = [own_tiles, exchange(own_tiles)]
        lists = product_lists(numbers, exchange(numbers), n_blocks)
        lines = share_lines(node_order, section_owner, send_blocks, tile_len)
        mine = features.at[lines.reshape(-1)].get(mode="promise_in_bounds")
        mine = mine.reshape(-1, tile_len, width)
        early, late, lists = gather_small(mine, section_owner, lists)
        parts = [part + [exchange(piece) for piece in part] for part in (early, late)]
        ends, place = [], 0
        for part in parts:
            ends.append([])
            for piece in part:
                ends[-1].append(place)
                place += piece.shape[0]
        hidden = products_in_phases(parts, ends, tile_list, lists, weight, n_blocks)
    else:
        tile_list = lax.all_gather(own_tiles, "rep", axis=0, tiled=True)
        numbers = lax.all_gather(numbers, "rep", axis=0)
        rows = (numbers[:, 0] - rep * n_blocks).reshape(-1)
        lines = share_rows(node_order, section_owner, send_blocks, tile_len)
        mine = features.at[lines.reshape(-1)].get(mode="promise_in_bounds")
        landed = lax.all_to_all(mine, "dom", 0, 0, tiled=True)
        landed = landed.reshape(n_dom, -1, width)
        shard = landed.at[section_owner].get(mode="promise_in_bounds")
        whole = lax.all_gather(shard, ("rep", "dom"), axis=0)
        whole = whole.transpose(1, 0, 2, 3).reshape(sections * n_send, tile_len, width)
        slots = jnp.arange(sections)[:, None] * n_send + numbers[:, 1]
        hidden = products(
            [whole], [0], tile_list, rows, slots.reshape(-1), weight, sections * n_send, n_blocks
        )
    return hidden.reshape(n_blocks * tile_len, -1)


def solution(mesh):
    return jax.shard_map(
        body,
        mesh=mesh,
        in_specs=(
            P("dom", None),
            P("dom", None),
            P(),
            P(),
            P("dom", None, "rep"),
            P("dom", None, "rep"),
            P("dom", None, "rep", None, None),
            P(),
        ),
        out_specs=P(("dom", "rep"), None),
        check_vma=False,
    )
```

```python
import functools

import jax
import jax.numpy as jnp
from jax import lax
from jax.experimental import pallas as pl
from jax.experimental.pallas import tpu as pltpu
from jax.sharding import PartitionSpec as P


UNROLL = 8


def load(n_first, pieces, places, sent, sem):
    return [
        pltpu.make_async_copy(piece, sent.at[pl.ds(place, piece.shape[0])], sem.at[n_first + i])
        for i, (piece, place) in enumerate(zip(pieces, places))
    ]


def put(lists, count, here, tile, row, place):
    lists[0, count] = tile
    lists[1, count] = row
    lists[2, count] = place
    return count + here.astype(jnp.int32)


def pad(lists, first, count, n_blocks):
    for i in range(UNROLL):
        put(lists, first + count + i, count >= 0, 0, n_blocks, 0)
    return (count + UNROLL - 1) // UNROLL


def run(lists, first, groups, tiles, sent, acc):
    def step(group, carry):
        at = [first + group * UNROLL + i for i in range(UNROLL)]
        done = [
            jnp.dot(
                tiles[lists[0, i]], sent[lists[2, i]], preferred_element_type=jnp.float32
            )
            for i in at
        ]
        for i, product in zip(at, done):
            acc[lists[1, i]] += product
        return carry

    lax.fori_loop(0, groups, step, 0)


def finish(acc, weight_ref, out_ref, stage, out_sem):
    steps, group, tile_len = stage.shape[:3]
    copies = []
    for i in range(steps):
        total = acc[pl.ds(i * group, group)].reshape(group * tile_len, acc.shape[2])
        mixed = jnp.dot(
            total.astype(jnp.bfloat16), weight_ref[...], preferred_element_type=jnp.float32
        )
        stage[i] = jnp.maximum(mixed, 0.0).astype(out_ref.dtype).reshape(stage.shape[1:])
        copies.append(
            pltpu.make_async_copy(stage.at[i], out_ref.at[pl.ds(i * group, group)], out_sem.at[i])
        )
        copies[-1].start()
    for copy in copies:
        copy.wait()


def whole_kernel(places, rows_ref, slots_ref, *refs):
    n = len(places)
    tile_ref, weight_ref, out_ref, sent, tiles, acc, stage, lists, sem, out_sem = refs[n:]
    n_tiles, n_blocks = rows_ref.shape[0], out_ref.shape[0]
    copies = load(0, refs[:n], places, sent, sem)
    copies.append(pltpu.make_async_copy(tile_ref, tiles, sem.at[n]))
    for copy in copies:
        copy.start()
    acc[...] = jnp.zeros_like(acc)

    def pick(t, count):
        row = rows_ref[t]
        here = jnp.logical_and(row >= 0, row < n_blocks)
        return put(lists, count, here, t, row, slots_ref[t])

    groups = pad(lists, 0, lax.fori_loop(0, n_tiles, pick, jnp.int32(0)), n_blocks)
    for copy in copies:
        copy.wait()
    run(lists, 0, groups, tiles, sent, acc)
    finish(acc, weight_ref, out_ref, stage, out_sem)


def phased_kernel(places, lists, *refs):
    counts = [len(part) for part in places]
    n = sum(counts)
    pieces, tile_refs = refs[:n], refs[n : n + 2]
    weight_ref, out_ref, sent, tiles, acc, stage, sem, out_sem = refs[n + 2 :]
    each = tiles.shape[0] // 2
    copies = [
        pltpu.make_async_copy(ref, tiles.at[pl.ds(i * each, each)], sem.at[n + i])
        for i, ref in enumerate(tile_refs)
    ]
    copies += load(0, pieces[: counts[0]], places[0], sent, sem)
    later = load(counts[0], pieces[counts[0] :], places[1], sent, sem)
    for copy in copies + later:
        copy.start()
    acc[...] = jnp.zeros_like(acc)
    middle = lists.shape[1] // 2
    for copy in copies:
        copy.wait()
    run(lists, 0, lists[3, 0], tiles, sent, acc)
    for copy in later:
        copy.wait()
    run(lists, middle, lists[3, middle], tiles, sent, acc)
    finish(acc, weight_ref, out_ref, stage, out_sem)


def lists_kernel(n_blocks, own_ref, other_ref, lists):
    me, rep = lax.axis_index("dom"), lax.axis_index("rep")
    sections, each = own_ref.shape[1:]
    middle = lists.shape[1] // 2
    early, late = jnp.int32(0), jnp.int32(0)
    for s in range(sections):
        for part, ref in enumerate((own_ref, other_ref)):

            def pick(k, counts, ref=ref, part=part, s=s):
                early, late = counts
                row = ref[0, s, k] - rep * n_blocks
                here = jnp.logical_and(row >= 0, row < n_blocks)
                col = ref[1, s, k]
                holder, chip = col // 16, col % 16
                other = (holder != rep).astype(jnp.int32)
                shift = (chip // 4 - me // 4) & 3
                at = place_of((chip ^ me) & 3, holder) * sections + s
                at = jnp.where((shift & 1) == 1, 4 * sections + at + (at // 4 + shift // 2) * 4, at)
                is_late = shift == 2
                place = jnp.where(is_late, 96 + other * 16 + at, other * 48 + at)
                put(
                    lists,
                    jnp.where(is_late, middle + late, early),
                    here,
                    (part * sections + s) * each + k,
                    row,
                    place,
                )
                now = here.astype(jnp.int32)
                return early + jnp.where(is_late, 0, now), late + jnp.where(is_late, now, 0)

            early, late = lax.fori_loop(0, each, pick, (early, late))
    lists[3, 0] = pad(lists, 0, early, n_blocks)
    lists[3, middle] = pad(lists, middle, late, n_blocks)


HBM = pl.BlockSpec(memory_space=pltpu.HBM)
SMEM = pl.BlockSpec(memory_space=pltpu.SMEM)
VMEM = pl.BlockSpec(memory_space=pltpu.VMEM)


def settings(n_products, tile_len, width, n_bytes):
    return {
        "compiler_params": pltpu.CompilerParams(vmem_limit_bytes=60 * 1024 * 1024),
        "cost_estimate": pl.CostEstimate(
            flops=2 * n_products * tile_len * tile_len * width,
            bytes_accessed=n_bytes,
            transcendentals=0,
        ),
    }


def out_stage(n_blocks, tile_len, width):
    group = min(4, n_blocks)
    return pltpu.VMEM((n_blocks // group, group, tile_len, width), jnp.bfloat16)


def products(pieces, places, tiles, rows, slots, weight, n_sent, n_blocks):
    n_tiles, tile_len = tiles.shape[:2]
    width = weight.shape[0]
    return pl.pallas_call(
        functools.partial(whole_kernel, tuple(places)),
        out_shape=jax.ShapeDtypeStruct((n_blocks, tile_len, weight.shape[1]), jnp.bfloat16),
        in_specs=[SMEM, SMEM] + [HBM] * (len(pieces) + 1) + [VMEM],
        out_specs=HBM,
        scratch_shapes=[
            pltpu.VMEM((n_sent, tile_len, width), jnp.bfloat16),
            pltpu.VMEM(tiles.shape, jnp.bfloat16),
            pltpu.VMEM((n_blocks + 1, tile_len, width), jnp.float32),
            out_stage(n_blocks, tile_len, weight.shape[1]),
            pltpu.SMEM((3, n_tiles + UNROLL), jnp.int32),
            pltpu.SemaphoreType.DMA((len(pieces) + 1,)),
            pltpu.SemaphoreType.DMA((n_blocks // min(4, n_blocks),)),
        ],
        **settings(n_tiles, tile_len, width, 16 << 20),
    )(rows, slots, *pieces, tiles, weight)


def products_in_phases(pieces, places, tile_list, lists, weight, n_blocks):
    n_tiles, tile_len = 2 * tile_list[0].shape[0], tile_list[0].shape[1]
    width = weight.shape[0]
    flat = pieces[0] + pieces[1]
    n_sent = sum(piece.shape[0] for piece in flat)
    return pl.pallas_call(
        functools.partial(phased_kernel, places),
        out_shape=jax.ShapeDtypeStruct((n_blocks, tile_len, weight.shape[1]), jnp.bfloat16),
        in_specs=[SMEM] + [HBM] * (len(flat) + 2) + [VMEM],
        out_specs=HBM,
        scratch_shapes=[
            pltpu.VMEM((n_sent, tile_len, width), jnp.bfloat16),
            pltpu.VMEM((n_tiles, tile_len, tile_len), jnp.bfloat16),
            pltpu.VMEM((n_blocks + 1, tile_len, width), jnp.float32),
            out_stage(n_blocks, tile_len, weight.shape[1]),
            pltpu.SemaphoreType.DMA((len(flat) + 2,)),
            pltpu.SemaphoreType.DMA((n_blocks // min(4, n_blocks),)),
        ],
        **settings(n_tiles, tile_len, width, 16 << 20),
    )(lists, *flat, *tile_list, weight)


def product_lists(own, other, n_blocks):
    n_tiles = 2 * own.shape[1] * own.shape[2]
    return pl.pallas_call(
        functools.partial(lists_kernel, n_blocks),
        out_shape=jax.ShapeDtypeStruct((4, 2 * (n_tiles + UNROLL)), jnp.int32),
        in_specs=[SMEM] * 2,
        out_specs=SMEM,
    )(own, other)


CHUNKS = 8
ROWS = 16


def pick_kernel(owner_ref, blocks_ref, order_ref, features_ref, out_ref, *scratch):
    lines, held, wide, line_sem, sem = scratch
    me, rep = lax.axis_index("dom"), lax.axis_index("rep")
    section = jnp.int32(0)
    for s in range(blocks_ref.shape[0]):
        section = jnp.where(owner_ref[s] == me, s, section)
    share, tile_len = out_ref.shape[:2]
    size = held.shape[0] // CHUNKS
    copies = [
        pltpu.make_async_copy(
            order_ref.at[blocks_ref[section, rep * share + j]], lines.at[j], line_sem.at[j]
        )
        for j in range(share)
    ]
    chunks = [
        pltpu.make_async_copy(
            features_ref.at[pl.ds(i * size, size)], held.at[pl.ds(i * size, size)], sem.at[i]
        )
        for i in range(CHUNKS)
    ]
    for copy in copies + chunks:
        copy.start()
    for i, copy in enumerate(chunks):
        copy.wait()
        wide[pl.ds(i * size, size)] = held[pl.ds(i * size, size)].astype(jnp.float32)
    for copy in copies:
        copy.wait()

    def one_block(j, carry):
        for first in range(0, tile_len, ROWS):
            rows = [wide[pl.ds(lines[j, 0, first + u], 1), :] for u in range(ROWS)]
            rows = jnp.concatenate(rows, axis=0).astype(out_ref.dtype)
            out_ref[j, pl.ds(first, ROWS), :] = rows
        return carry

    lax.fori_loop(0, share, one_block, 0)


def pick_share(features, node_order, section_owner, send_blocks, tile_len):
    rows, width = features.shape
    share = send_blocks.shape[1] // 2
    return pl.pallas_call(
        pick_kernel,
        out_shape=jax.ShapeDtypeStruct((share, tile_len, width), features.dtype),
        in_specs=[SMEM, SMEM, HBM, HBM],
        out_specs=VMEM,
        scratch_shapes=[
            pltpu.SMEM((share, 1, tile_len), jnp.int32),
            pltpu.VMEM((rows, width), features.dtype),
            pltpu.VMEM((rows, width), jnp.float32),
            pltpu.SemaphoreType.DMA((share,)),
            pltpu.SemaphoreType.DMA((CHUNKS,)),
        ],
        compiler_params=pltpu.CompilerParams(vmem_limit_bytes=60 * 1024 * 1024),
    )(section_owner, send_blocks, node_order[0].reshape(-1, 1, tile_len), features)


def share_rows(node_order, section_owner, send_blocks, tile_len):
    me = lax.axis_index("dom")
    sections, n_send = send_blocks.shape
    mine = (section_owner == me).astype(jnp.int32)
    section = jnp.sum(mine * jnp.arange(sections, dtype=jnp.int32))
    share = n_send // lax.axis_size("rep")
    picks = lax.dynamic_slice(
        send_blocks, (section, lax.axis_index("rep") * share), (1, share)
    )[0]
    order = node_order[0].reshape(-1, tile_len)
    return order.at[picks].get(mode="promise_in_bounds")


def move(value, pairs):
    return lax.ppermute(value, "dom", pairs)


def flip(bits):
    return [(i, i ^ bits) for i in range(16)]


def cross(value, turn):
    pairs = []
    for i in range(16):
        for core in (0, 1):
            pairs.append((2 * i + core, 2 * (i ^ (1 if core == turn else 2)) + core))
    return lax.ppermute(value, ("dom", "rep"), pairs)


def place_of(across, core):
    return jnp.where(core == 0, across, (across & 1) * 2 + across // 2)


def tie(value, after):
    return lax.optimization_barrier((value, after))[0]


def quad_gather(own):
    came = cross(own, 0)
    pair = jnp.concatenate([own, came])
    return came, [pair, cross(pair, 1)]


RING = {
    k: [(z * 4 + q, ((z - k) % 4) * 4 + q) for z in range(4) for q in range(4)] for k in (1, 2, 3)
}


def gather_small(rows, section_owner, lists):
    landed = lax.all_to_all(rows, "dom", 0, 0, tiled=True)
    shard = landed.at[section_owner].get(mode="promise_in_bounds")
    shard, lists = lax.optimization_barrier((shard, lists))
    one = move(shard, RING[1])
    near = jnp.concatenate([one, move(shard, RING[3])])
    came, level = quad_gather(shard)
    far = move(one, RING[1])
    near_came, near_level = quad_gather(tie(near, came))
    near_level[1] = cross(tie(near_level[0], (far, level[1])), 1)
    return level + near_level, quad_gather(far)[1], lists


def body(features, node_order, section_owner, send_blocks, tile_rows, tile_cols, tiles, weight):
    width = features.shape[1]
    tile_len = tiles.shape[3]
    blocks = features.shape[0] // tile_len
    n_dom, n_rep = lax.axis_size("dom"), lax.axis_size("rep")
    sections, n_send = send_blocks.shape
    me, rep = lax.axis_index("dom"), lax.axis_index("rep")
    n_blocks = blocks // n_rep
    small = n_dom == 16 and n_rep == 2 and n_send == n_dom * n_rep

    own_tiles = tiles[0].reshape(-1, tile_len, tile_len)
    numbers = jnp.stack([tile_rows[0], tile_cols[0]])
    if small:
        swap = [(0, 1), (1, 0)]

        def exchange(value):
            return lax.ppermute(value, "rep", swap)

        tile_list = [own_tiles, exchange(own_tiles)]
        lists = product_lists(numbers, exchange(numbers), n_blocks)
        mine = pick_share(features, node_order, section_owner, send_blocks, tile_len)
        early, late, lists = gather_small(mine, section_owner, lists)
        parts = [part + [exchange(piece) for piece in part] for part in (early, late)]
        ends, place = [], 0
        for part in parts:
            ends.append([])
            for piece in part:
                ends[-1].append(place)
                place += piece.shape[0]
        hidden = products_in_phases(parts, ends, tile_list, lists, weight, n_blocks)
    else:
        tile_list = lax.all_gather(own_tiles, "rep", axis=0, tiled=True)
        numbers = lax.all_gather(numbers, "rep", axis=0)
        rows = (numbers[:, 0] - rep * n_blocks).reshape(-1)
        lines = share_rows(node_order, section_owner, send_blocks, tile_len)
        mine = features.at[lines.reshape(-1)].get(mode="promise_in_bounds")
        landed = lax.all_to_all(mine, "dom", 0, 0, tiled=True)
        landed = landed.reshape(n_dom, -1, width)
        shard = landed.at[section_owner].get(mode="promise_in_bounds")
        whole = lax.all_gather(shard, ("rep", "dom"), axis=0)
        whole = whole.transpose(1, 0, 2, 3).reshape(sections * n_send, tile_len, width)
        slots = jnp.arange(sections)[:, None] * n_send + numbers[:, 1]
        hidden = products(
            [whole], [0], tile_list, rows, slots.reshape(-1), weight, sections * n_send, n_blocks
        )
    return hidden.reshape(n_blocks * tile_len, -1)


def solution(mesh):
    return jax.shard_map(
        body,
        mesh=mesh,
        in_specs=(
            P("dom", None),
            P("dom", None),
            P(),
            P(),
            P("dom", None, "rep"),
            P("dom", None, "rep"),
            P("dom", None, "rep", None, None),
            P(),
        ),
        out_specs=P(("dom", "rep"), None),
        check_vma=False,
    )
```

```python
import functools

import jax
import jax.numpy as jnp
from jax import lax
from jax.experimental import pallas as pl
from jax.experimental.pallas import tpu as pltpu
from jax.sharding import PartitionSpec as P


UNROLL = 8


def load(n_first, pieces, places, sent, sem):
    return [
        pltpu.make_async_copy(piece, sent.at[pl.ds(place, piece.shape[0])], sem.at[n_first + i])
        for i, (piece, place) in enumerate(zip(pieces, places))
    ]


def put(lists, count, here, tile, row, place):
    lists[0, count] = tile
    lists[1, count] = row
    lists[2, count] = place
    return count + here.astype(jnp.int32)


def pad(lists, first, count, n_blocks):
    for i in range(UNROLL):
        put(lists, first + count + i, count >= 0, 0, n_blocks, 0)
    return (count + UNROLL - 1) // UNROLL


def run(lists, first, groups, tiles, sent, acc):
    def step(group, carry):
        at = [first + group * UNROLL + i for i in range(UNROLL)]
        done = [
            jnp.dot(
                tiles[lists[0, i]], sent[lists[2, i]], preferred_element_type=jnp.float32
            )
            for i in at
        ]
        for i, product in zip(at, done):
            acc[lists[1, i]] += product
        return carry

    lax.fori_loop(0, groups, step, 0)


def finish(acc, weight_ref, out_ref, stage, out_sem):
    steps, group, tile_len = stage.shape[:3]
    copies = []
    for i in range(steps):
        total = acc[pl.ds(i * group, group)].reshape(group * tile_len, acc.shape[2])
        mixed = jnp.dot(
            total.astype(jnp.bfloat16), weight_ref[...], preferred_element_type=jnp.float32
        )
        stage[i] = jnp.maximum(mixed, 0.0).astype(out_ref.dtype).reshape(stage.shape[1:])
        copies.append(
            pltpu.make_async_copy(stage.at[i], out_ref.at[pl.ds(i * group, group)], out_sem.at[i])
        )
        copies[-1].start()
    for copy in copies:
        copy.wait()


def whole_kernel(places, rows_ref, slots_ref, *refs):
    n = len(places)
    tile_ref, weight_ref, out_ref, sent, tiles, acc, stage, lists, sem, out_sem = refs[n:]
    n_tiles, n_blocks = rows_ref.shape[0], out_ref.shape[0]
    copies = load(0, refs[:n], places, sent, sem)
    copies.append(pltpu.make_async_copy(tile_ref, tiles, sem.at[n]))
    for copy in copies:
        copy.start()
    acc[...] = jnp.zeros_like(acc)

    def pick(t, count):
        row = rows_ref[t]
        here = jnp.logical_and(row >= 0, row < n_blocks)
        return put(lists, count, here, t, row, slots_ref[t])

    groups = pad(lists, 0, lax.fori_loop(0, n_tiles, pick, jnp.int32(0)), n_blocks)
    for copy in copies:
        copy.wait()
    run(lists, 0, groups, tiles, sent, acc)
    finish(acc, weight_ref, out_ref, stage, out_sem)


def phased_kernel(places, lists, *refs):
    counts = [len(part) for part in places]
    n = sum(counts)
    pieces, tile_refs = refs[:n], refs[n : n + 2]
    weight_ref, out_ref, sent, tiles, acc, stage, sem, out_sem = refs[n + 2 :]
    each = tiles.shape[0] // 2
    copies = [
        pltpu.make_async_copy(ref, tiles.at[pl.ds(i * each, each)], sem.at[n + i])
        for i, ref in enumerate(tile_refs)
    ]
    copies += load(0, pieces[: counts[0]], places[0], sent, sem)
    later = load(counts[0], pieces[counts[0] :], places[1], sent, sem)
    for copy in copies + later:
        copy.start()
    acc[...] = jnp.zeros_like(acc)
    middle = lists.shape[1] // 2
    for copy in copies:
        copy.wait()
    run(lists, 0, lists[3, 0], tiles, sent, acc)
    for copy in later:
        copy.wait()
    run(lists, middle, lists[3, middle], tiles, sent, acc)
    finish(acc, weight_ref, out_ref, stage, out_sem)


def lists_kernel(n_blocks, own_ref, other_ref, lists):
    me, rep = lax.axis_index("dom"), lax.axis_index("rep")
    sections, each = own_ref.shape[1:]
    middle = lists.shape[1] // 2
    early, late = jnp.int32(0), jnp.int32(0)
    for s in range(sections):
        for part, ref in enumerate((own_ref, other_ref)):

            def pick(k, counts, ref=ref, part=part, s=s):
                early, late = counts
                row = ref[0, s, k] - rep * n_blocks
                here = jnp.logical_and(row >= 0, row < n_blocks)
                col = ref[1, s, k]
                holder, chip = col // 16, col % 16
                other = (holder != rep).astype(jnp.int32)
                shift = (chip // 4 - me // 4) & 3
                at = place_of((chip ^ me) & 3, holder) * sections + s
                turn, by_shift = at // 8, shift // 2
                near = 16 + jnp.where(
                    turn == 0, at + (at // 4) * 4 + by_shift * 4, 8 + at + by_shift * 8
                )
                at = jnp.where((shift & 1) == 1, near, at)
                is_late = shift == 2
                place = jnp.where(is_late, 96 + other * 16 + at, other * 48 + at)
                put(
                    lists,
                    jnp.where(is_late, middle + late, early),
                    here,
                    (part * sections + s) * each + k,
                    row,
                    place,
                )
                now = here.astype(jnp.int32)
                return early + jnp.where(is_late, 0, now), late + jnp.where(is_late, now, 0)

            early, late = lax.fori_loop(0, each, pick, (early, late))
    lists[3, 0] = pad(lists, 0, early, n_blocks)
    lists[3, middle] = pad(lists, middle, late, n_blocks)


HBM = pl.BlockSpec(memory_space=pltpu.HBM)
SMEM = pl.BlockSpec(memory_space=pltpu.SMEM)
VMEM = pl.BlockSpec(memory_space=pltpu.VMEM)


def settings(n_products, tile_len, width, n_bytes):
    return {
        "compiler_params": pltpu.CompilerParams(vmem_limit_bytes=60 * 1024 * 1024),
        "cost_estimate": pl.CostEstimate(
            flops=2 * n_products * tile_len * tile_len * width,
            bytes_accessed=n_bytes,
            transcendentals=0,
        ),
    }


def out_stage(n_blocks, tile_len, width):
    group = min(4, n_blocks)
    return pltpu.VMEM((n_blocks // group, group, tile_len, width), jnp.bfloat16)


def products(pieces, places, tiles, rows, slots, weight, n_sent, n_blocks):
    n_tiles, tile_len = tiles.shape[:2]
    width = weight.shape[0]
    return pl.pallas_call(
        functools.partial(whole_kernel, tuple(places)),
        out_shape=jax.ShapeDtypeStruct((n_blocks, tile_len, weight.shape[1]), jnp.bfloat16),
        in_specs=[SMEM, SMEM] + [HBM] * (len(pieces) + 1) + [VMEM],
        out_specs=HBM,
        scratch_shapes=[
            pltpu.VMEM((n_sent, tile_len, width), jnp.bfloat16),
            pltpu.VMEM(tiles.shape, jnp.bfloat16),
            pltpu.VMEM((n_blocks + 1, tile_len, width), jnp.float32),
            out_stage(n_blocks, tile_len, weight.shape[1]),
            pltpu.SMEM((3, n_tiles + UNROLL), jnp.int32),
            pltpu.SemaphoreType.DMA((len(pieces) + 1,)),
            pltpu.SemaphoreType.DMA((n_blocks // min(4, n_blocks),)),
        ],
        **settings(n_tiles, tile_len, width, 16 << 20),
    )(rows, slots, *pieces, tiles, weight)


def products_in_phases(pieces, places, tile_list, lists, weight, n_blocks):
    n_tiles, tile_len = 2 * tile_list[0].shape[0], tile_list[0].shape[1]
    width = weight.shape[0]
    flat = pieces[0] + pieces[1]
    n_sent = sum(piece.shape[0] for piece in flat)
    return pl.pallas_call(
        functools.partial(phased_kernel, places),
        out_shape=jax.ShapeDtypeStruct((n_blocks, tile_len, weight.shape[1]), jnp.bfloat16),
        in_specs=[SMEM] + [HBM] * (len(flat) + 2) + [VMEM],
        out_specs=HBM,
        scratch_shapes=[
            pltpu.VMEM((n_sent, tile_len, width), jnp.bfloat16),
            pltpu.VMEM((n_tiles, tile_len, tile_len), jnp.bfloat16),
            pltpu.VMEM((n_blocks + 1, tile_len, width), jnp.float32),
            out_stage(n_blocks, tile_len, weight.shape[1]),
            pltpu.SemaphoreType.DMA((len(flat) + 2,)),
            pltpu.SemaphoreType.DMA((n_blocks // min(4, n_blocks),)),
        ],
        **settings(n_tiles, tile_len, width, 16 << 20),
    )(lists, *flat, *tile_list, weight)


def product_lists(own, other, n_blocks):
    n_tiles = 2 * own.shape[1] * own.shape[2]
    return pl.pallas_call(
        functools.partial(lists_kernel, n_blocks),
        out_shape=jax.ShapeDtypeStruct((4, 2 * (n_tiles + UNROLL)), jnp.int32),
        in_specs=[SMEM] * 2,
        out_specs=SMEM,
    )(own, other)


CHUNKS = 8
ROWS = 16


def pick_kernel(owner_ref, blocks_ref, order_ref, features_ref, out_ref, *scratch):
    lines, held, wide, line_sem, sem = scratch
    me, rep = lax.axis_index("dom"), lax.axis_index("rep")
    section = jnp.int32(0)
    for s in range(blocks_ref.shape[0]):
        section = jnp.where(owner_ref[s] == me, s, section)
    share, tile_len = out_ref.shape[:2]
    size = held.shape[0] // CHUNKS
    copies = [
        pltpu.make_async_copy(
            order_ref.at[blocks_ref[section, rep * share + j]], lines.at[j], line_sem.at[j]
        )
        for j in range(share)
    ]
    chunks = [
        pltpu.make_async_copy(
            features_ref.at[pl.ds(i * size, size)], held.at[pl.ds(i * size, size)], sem.at[i]
        )
        for i in range(CHUNKS)
    ]
    for copy in copies + chunks:
        copy.start()
    for i, copy in enumerate(chunks):
        copy.wait()
        wide[pl.ds(i * size, size)] = held[pl.ds(i * size, size)].astype(jnp.float32)
    for copy in copies:
        copy.wait()

    def one_block(j, carry):
        for first in range(0, tile_len, ROWS):
            rows = [wide[pl.ds(lines[j, 0, first + u], 1), :] for u in range(ROWS)]
            rows = jnp.concatenate(rows, axis=0).astype(out_ref.dtype)
            out_ref[j, pl.ds(first, ROWS), :] = rows
        return carry

    lax.fori_loop(0, share, one_block, 0)


def pick_share(features, node_order, section_owner, send_blocks, tile_len):
    rows, width = features.shape
    share = send_blocks.shape[1] // 2
    return pl.pallas_call(
        pick_kernel,
        out_shape=jax.ShapeDtypeStruct((share, tile_len, width), features.dtype),
        in_specs=[SMEM, SMEM, HBM, HBM],
        out_specs=VMEM,
        scratch_shapes=[
            pltpu.SMEM((share, 1, tile_len), jnp.int32),
            pltpu.VMEM((rows, width), features.dtype),
            pltpu.VMEM((rows, width), jnp.float32),
            pltpu.SemaphoreType.DMA((share,)),
            pltpu.SemaphoreType.DMA((CHUNKS,)),
        ],
        compiler_params=pltpu.CompilerParams(vmem_limit_bytes=60 * 1024 * 1024),
    )(section_owner, send_blocks, node_order[0].reshape(-1, 1, tile_len), features)


def share_rows(node_order, section_owner, send_blocks, tile_len):
    me = lax.axis_index("dom")
    sections, n_send = send_blocks.shape
    mine = (section_owner == me).astype(jnp.int32)
    section = jnp.sum(mine * jnp.arange(sections, dtype=jnp.int32))
    share = n_send // lax.axis_size("rep")
    picks = lax.dynamic_slice(
        send_blocks, (section, lax.axis_index("rep") * share), (1, share)
    )[0]
    order = node_order[0].reshape(-1, tile_len)
    return order.at[picks].get(mode="promise_in_bounds")


def move(value, pairs):
    return lax.ppermute(value, "dom", pairs)


def flip(bits):
    return [(i, i ^ bits) for i in range(16)]


def cross(value, turn):
    pairs = []
    for i in range(16):
        for core in (0, 1):
            pairs.append((2 * i + core, 2 * (i ^ (1 if core == turn else 2)) + core))
    return lax.ppermute(value, ("dom", "rep"), pairs)


def place_of(across, core):
    return jnp.where(core == 0, across, (across & 1) * 2 + across // 2)


def tie(value, after):
    return lax.optimization_barrier((value, after))[0]


RING = {
    k: [(z * 4 + q, ((z - k) % 4) * 4 + q) for z in range(4) for q in range(4)] for k in (1, 2, 3)
}


def gather_small(rows, section_owner, lists):
    landed = lax.all_to_all(rows, "dom", 0, 0, tiled=True)
    shard = landed.at[section_owner].get(mode="promise_in_bounds")
    shard, lists = lax.optimization_barrier((shard, lists))
    one, three = move(shard, RING[1]), move(shard, RING[3])
    came, turned = cross(shard, 0), cross(shard, 1)
    second = jnp.concatenate([turned, cross(came, 1)])
    near = jnp.concatenate([one, three])
    far = move(one, RING[1])
    one_second = move(second, RING[1])
    near_came = cross(tie(near, (came, turned)), 0)
    each = shard.shape[0]
    three_second = cross(jnp.concatenate([three, near_came[each:]]), 1)
    far_pair = jnp.concatenate([far, cross(far, 0)])
    early = [shard, came, second, near, near_came, one_second, three_second]
    return early, [far_pair, cross(tie(far_pair, (one_second, three_second)), 1)], lists


def body(features, node_order, section_owner, send_blocks, tile_rows, tile_cols, tiles, weight):
    width = features.shape[1]
    tile_len = tiles.shape[3]
    blocks = features.shape[0] // tile_len
    n_dom, n_rep = lax.axis_size("dom"), lax.axis_size("rep")
    sections, n_send = send_blocks.shape
    me, rep = lax.axis_index("dom"), lax.axis_index("rep")
    n_blocks = blocks // n_rep
    small = n_dom == 16 and n_rep == 2 and n_send == n_dom * n_rep

    own_tiles = tiles[0].reshape(-1, tile_len, tile_len)
    numbers = jnp.stack([tile_rows[0], tile_cols[0]])
    if small:
        swap = [(0, 1), (1, 0)]

        def exchange(value):
            return lax.ppermute(value, "rep", swap)

        tile_list = [own_tiles, exchange(own_tiles)]
        lists = product_lists(numbers, exchange(numbers), n_blocks)
        mine = pick_share(features, node_order, section_owner, send_blocks, tile_len)
        early, late, lists = gather_small(mine, section_owner, lists)
        parts = [part + [exchange(piece) for piece in part] for part in (early, late)]
        ends, place = [], 0
        for part in parts:
            ends.append([])
            for piece in part:
                ends[-1].append(place)
                place += piece.shape[0]
        hidden = products_in_phases(parts, ends, tile_list, lists, weight, n_blocks)
    else:
        tile_list = lax.all_gather(own_tiles, "rep", axis=0, tiled=True)
        numbers = lax.all_gather(numbers, "rep", axis=0)
        rows = (numbers[:, 0] - rep * n_blocks).reshape(-1)
        lines = share_rows(node_order, section_owner, send_blocks, tile_len)
        mine = features.at[lines.reshape(-1)].get(mode="promise_in_bounds")
        landed = lax.all_to_all(mine, "dom", 0, 0, tiled=True)
        landed = landed.reshape(n_dom, -1, width)
        shard = landed.at[section_owner].get(mode="promise_in_bounds")
        whole = lax.all_gather(shard, ("rep", "dom"), axis=0)
        whole = whole.transpose(1, 0, 2, 3).reshape(sections * n_send, tile_len, width)
        slots = jnp.arange(sections)[:, None] * n_send + numbers[:, 1]
        hidden = products(
            [whole], [0], tile_list, rows, slots.reshape(-1), weight, sections * n_send, n_blocks
        )
    return hidden.reshape(n_blocks * tile_len, -1)


def solution(mesh):
    return jax.shard_map(
        body,
        mesh=mesh,
        in_specs=(
            P("dom", None),
            P("dom", None),
            P(),
            P(),
            P("dom", None, "rep"),
            P("dom", None, "rep"),
            P("dom", None, "rep", None, None),
            P(),
        ),
        out_specs=P(("dom", "rep"), None),
        check_vma=False,
    )
```

```python
import functools

import jax
import jax.numpy as jnp
from jax import lax
from jax.experimental import pallas as pl
from jax.experimental.pallas import tpu as pltpu
from jax.sharding import PartitionSpec as P


UNROLL = 8


def load(n_first, pieces, places, sent, sem):
    return [
        pltpu.make_async_copy(piece, sent.at[pl.ds(place, piece.shape[0])], sem.at[n_first + i])
        for i, (piece, place) in enumerate(zip(pieces, places))
    ]


def put(lists, count, here, tile, row, place):
    lists[0, count] = tile
    lists[1, count] = row
    lists[2, count] = place
    return count + here.astype(jnp.int32)


def pad(lists, first, count, n_blocks):
    for i in range(UNROLL):
        put(lists, first + count + i, count >= 0, 0, n_blocks, 0)
    return (count + UNROLL - 1) // UNROLL


def run(lists, first, groups, tiles, sent, acc):
    def step(group, carry):
        at = [first + group * UNROLL + i for i in range(UNROLL)]
        done = [
            jnp.dot(
                tiles[lists[0, i]], sent[lists[2, i]], preferred_element_type=jnp.float32
            )
            for i in at
        ]
        for i, product in zip(at, done):
            acc[lists[1, i]] += product
        return carry

    lax.fori_loop(0, groups, step, 0)


def finish(acc, weight_ref, out_ref, stage, out_sem):
    steps, group, tile_len = stage.shape[:3]
    copies = []
    for i in range(steps):
        total = acc[pl.ds(i * group, group)].reshape(group * tile_len, acc.shape[2])
        mixed = jnp.dot(
            total.astype(jnp.bfloat16), weight_ref[...], preferred_element_type=jnp.float32
        )
        stage[i] = jnp.maximum(mixed, 0.0).astype(out_ref.dtype).reshape(stage.shape[1:])
        copies.append(
            pltpu.make_async_copy(stage.at[i], out_ref.at[pl.ds(i * group, group)], out_sem.at[i])
        )
        copies[-1].start()
    for copy in copies:
        copy.wait()


def whole_kernel(places, rows_ref, slots_ref, *refs):
    n = len(places)
    tile_ref, weight_ref, out_ref, sent, tiles, acc, stage, lists, sem, out_sem = refs[n:]
    n_tiles, n_blocks = rows_ref.shape[0], out_ref.shape[0]
    copies = load(0, refs[:n], places, sent, sem)
    copies.append(pltpu.make_async_copy(tile_ref, tiles, sem.at[n]))
    for copy in copies:
        copy.start()
    acc[...] = jnp.zeros_like(acc)

    def pick(t, count):
        row = rows_ref[t]
        here = jnp.logical_and(row >= 0, row < n_blocks)
        return put(lists, count, here, t, row, slots_ref[t])

    groups = pad(lists, 0, lax.fori_loop(0, n_tiles, pick, jnp.int32(0)), n_blocks)
    for copy in copies:
        copy.wait()
    run(lists, 0, groups, tiles, sent, acc)
    finish(acc, weight_ref, out_ref, stage, out_sem)


def phased_kernel(places, lists, *refs):
    n = sum(len(part) for part in places)
    pieces, tile_refs = refs[:n], refs[n : n + 2]
    weight_ref, out_ref, sent, tiles, acc, stage, sem, out_sem = refs[n + 2 :]
    each = tiles.shape[0] // 2
    copies, at = [], 0
    for part in places:
        copies.append(load(at, pieces[at : at + len(part)], part, sent, sem))
        at += len(part)
    copies[0] += [
        pltpu.make_async_copy(ref, tiles.at[pl.ds(i * each, each)], sem.at[n + i])
        for i, ref in enumerate(tile_refs)
    ]
    for copy in copies[0]:
        copy.start()
    acc[...] = jnp.zeros_like(acc)
    for part in copies[1:]:
        for copy in part:
            copy.start()
    span = lists.shape[1] // len(places)
    for i, part in enumerate(copies):
        for copy in part:
            copy.wait()
        run(lists, i * span, lists[3, i * span], tiles, sent, acc)
    finish(acc, weight_ref, out_ref, stage, out_sem)


def lists_kernel(n_blocks, own_ref, other_ref, lists):
    me, rep = lax.axis_index("dom"), lax.axis_index("rep")
    sections, each = own_ref.shape[1:]
    span = lists.shape[1] // 3
    counts = (jnp.int32(0),) * 3
    for s in range(sections):
        for part, ref in enumerate((own_ref, other_ref)):

            def pick(k, counts, ref=ref, part=part, s=s):
                row = ref[0, s, k] - rep * n_blocks
                here = jnp.logical_and(row >= 0, row < n_blocks)
                col = ref[1, s, k]
                holder, chip = col // 16, col % 16
                other = (holder != rep).astype(jnp.int32)
                shift = (chip // 4 - me // 4) & 3
                turn = place_of((chip ^ me) & 3, holder)
                at = turn * sections + s
                by_shift = shift // 2
                near = jnp.where(
                    turn < 2, at + (turn + by_shift) * 4, 8 + at + by_shift * 8
                )
                place = jnp.where(shift == 0, other * 16 + at, 96 + other * 16 + at)
                place = jnp.where((shift & 1) == 1, 32 + other * 32 + near, place)
                phase = jnp.where((shift & 1) == 1, 1, shift)
                target = jnp.where(
                    phase == 0,
                    counts[0],
                    jnp.where(phase == 1, span + counts[1], 2 * span + counts[2]),
                )
                put(lists, target, here, (part * sections + s) * each + k, row, place)
                now = here.astype(jnp.int32)
                return tuple(c + jnp.where(phase == i, now, 0) for i, c in enumerate(counts))

            counts = lax.fori_loop(0, each, pick, counts)
    for i, count in enumerate(counts):
        lists[3, i * span] = pad(lists, i * span, count, n_blocks)


HBM = pl.BlockSpec(memory_space=pltpu.HBM)
SMEM = pl.BlockSpec(memory_space=pltpu.SMEM)
VMEM = pl.BlockSpec(memory_space=pltpu.VMEM)


def settings(n_products, tile_len, width, n_bytes):
    return {
        "compiler_params": pltpu.CompilerParams(vmem_limit_bytes=60 * 1024 * 1024),
        "cost_estimate": pl.CostEstimate(
            flops=2 * n_products * tile_len * tile_len * width,
            bytes_accessed=n_bytes,
            transcendentals=0,
        ),
    }


def out_stage(n_blocks, tile_len, width):
    group = min(4, n_blocks)
    return pltpu.VMEM((n_blocks // group, group, tile_len, width), jnp.bfloat16)


def products(pieces, places, tiles, rows, slots, weight, n_sent, n_blocks):
    n_tiles, tile_len = tiles.shape[:2]
    width = weight.shape[0]
    return pl.pallas_call(
        functools.partial(whole_kernel, tuple(places)),
        out_shape=jax.ShapeDtypeStruct((n_blocks, tile_len, weight.shape[1]), jnp.bfloat16),
        in_specs=[SMEM, SMEM] + [HBM] * (len(pieces) + 1) + [VMEM],
        out_specs=HBM,
        scratch_shapes=[
            pltpu.VMEM((n_sent, tile_len, width), jnp.bfloat16),
            pltpu.VMEM(tiles.shape, jnp.bfloat16),
            pltpu.VMEM((n_blocks + 1, tile_len, width), jnp.float32),
            out_stage(n_blocks, tile_len, weight.shape[1]),
            pltpu.SMEM((3, n_tiles + UNROLL), jnp.int32),
            pltpu.SemaphoreType.DMA((len(pieces) + 1,)),
            pltpu.SemaphoreType.DMA((n_blocks // min(4, n_blocks),)),
        ],
        **settings(n_tiles, tile_len, width, 16 << 20),
    )(rows, slots, *pieces, tiles, weight)


def products_in_phases(pieces, places, tile_list, lists, weight, n_blocks):
    n_tiles, tile_len = 2 * tile_list[0].shape[0], tile_list[0].shape[1]
    width = weight.shape[0]
    flat = [piece for part in pieces for piece in part]
    n_sent = sum(piece.shape[0] for piece in flat)
    return pl.pallas_call(
        functools.partial(phased_kernel, places),
        out_shape=jax.ShapeDtypeStruct((n_blocks, tile_len, weight.shape[1]), jnp.bfloat16),
        in_specs=[SMEM] + [HBM] * (len(flat) + 2) + [VMEM],
        out_specs=HBM,
        scratch_shapes=[
            pltpu.VMEM((n_sent, tile_len, width), jnp.bfloat16),
            pltpu.VMEM((n_tiles, tile_len, tile_len), jnp.bfloat16),
            pltpu.VMEM((n_blocks + 1, tile_len, width), jnp.float32),
            out_stage(n_blocks, tile_len, weight.shape[1]),
            pltpu.SemaphoreType.DMA((len(flat) + 2,)),
            pltpu.SemaphoreType.DMA((n_blocks // min(4, n_blocks),)),
        ],
        **settings(n_tiles, tile_len, width, 16 << 20),
    )(lists, *flat, *tile_list, weight)


def product_lists(own, other, n_blocks):
    n_tiles = 2 * own.shape[1] * own.shape[2]
    return pl.pallas_call(
        functools.partial(lists_kernel, n_blocks),
        out_shape=jax.ShapeDtypeStruct((4, 3 * (n_tiles + UNROLL)), jnp.int32),
        in_specs=[SMEM] * 2,
        out_specs=SMEM,
    )(own, other)


CHUNKS = 8
ROWS = 16


def pick_kernel(owner_ref, blocks_ref, order_ref, features_ref, out_ref, *scratch):
    lines, held, wide, line_sem, sem = scratch
    me, rep = lax.axis_index("dom"), lax.axis_index("rep")
    section = jnp.int32(0)
    for s in range(blocks_ref.shape[0]):
        section = jnp.where(owner_ref[s] == me, s, section)
    share, tile_len = out_ref.shape[:2]
    size = held.shape[0] // CHUNKS
    copies = [
        pltpu.make_async_copy(
            order_ref.at[blocks_ref[section, rep * share + j]], lines.at[j], line_sem.at[j]
        )
        for j in range(share)
    ]
    chunks = [
        pltpu.make_async_copy(
            features_ref.at[pl.ds(i * size, size)], held.at[pl.ds(i * size, size)], sem.at[i]
        )
        for i in range(CHUNKS)
    ]
    for copy in copies + chunks:
        copy.start()
    for i, copy in enumerate(chunks):
        copy.wait()
        wide[pl.ds(i * size, size)] = held[pl.ds(i * size, size)].astype(jnp.float32)
    for copy in copies:
        copy.wait()

    def one_block(j, carry):
        for first in range(0, tile_len, ROWS):
            rows = [wide[pl.ds(lines[j, 0, first + u], 1), :] for u in range(ROWS)]
            rows = jnp.concatenate(rows, axis=0).astype(out_ref.dtype)
            out_ref[j, pl.ds(first, ROWS), :] = rows
        return carry

    lax.fori_loop(0, share, one_block, 0)


def pick_share(features, node_order, section_owner, send_blocks, tile_len):
    rows, width = features.shape
    share = send_blocks.shape[1] // 2
    return pl.pallas_call(
        pick_kernel,
        out_shape=jax.ShapeDtypeStruct((share, tile_len, width), features.dtype),
        in_specs=[SMEM, SMEM, HBM, HBM],
        out_specs=VMEM,
        scratch_shapes=[
            pltpu.SMEM((share, 1, tile_len), jnp.int32),
            pltpu.VMEM((rows, width), features.dtype),
            pltpu.VMEM((rows, width), jnp.float32),
            pltpu.SemaphoreType.DMA((share,)),
            pltpu.SemaphoreType.DMA((CHUNKS,)),
        ],
        compiler_params=pltpu.CompilerParams(vmem_limit_bytes=60 * 1024 * 1024),
    )(section_owner, send_blocks, node_order[0].reshape(-1, 1, tile_len), features)


def share_rows(node_order, section_owner, send_blocks, tile_len):
    me = lax.axis_index("dom")
    sections, n_send = send_blocks.shape
    mine = (section_owner == me).astype(jnp.int32)
    section = jnp.sum(mine * jnp.arange(sections, dtype=jnp.int32))
    share = n_send // lax.axis_size("rep")
    picks = lax.dynamic_slice(
        send_blocks, (section, lax.axis_index("rep") * share), (1, share)
    )[0]
    order = node_order[0].reshape(-1, tile_len)
    return order.at[picks].get(mode="promise_in_bounds")


def move(value, pairs):
    return lax.ppermute(value, "dom", pairs)


def flip(bits):
    return [(i, i ^ bits) for i in range(16)]


def cross(value, turn):
    pairs = []
    for i in range(16):
        for core in (0, 1):
            pairs.append((2 * i + core, 2 * (i ^ (1 if core == turn else 2)) + core))
    return lax.ppermute(value, ("dom", "rep"), pairs)


def place_of(across, core):
    return jnp.where(core == 0, across, (across & 1) * 2 + across // 2)


def tie(value, after):
    return lax.optimization_barrier((value, after))[0]


RING = {
    k: [(z * 4 + q, ((z - k) % 4) * 4 + q) for z in range(4) for q in range(4)] for k in (1, 2, 3)
}


def gather_small(rows, section_owner, lists):
    landed = lax.all_to_all(rows, "dom", 0, 0, tiled=True)
    shard = landed.at[section_owner].get(mode="promise_in_bounds")
    shard, lists = lax.optimization_barrier((shard, lists))
    one, three = move(shard, RING[1]), move(shard, RING[3])
    came, turned = cross(shard, 0), cross(shard, 1)
    second = jnp.concatenate([turned, cross(came, 1)])
    near = jnp.concatenate([one, three])
    far = move(one, RING[1])
    one_second = move(second, RING[1])
    near_came = cross(tie(near, (came, turned)), 0)
    each = shard.shape[0]
    three_second = cross(jnp.concatenate([three, near_came[each:]]), 1)
    far_pair = jnp.concatenate([far, cross(far, 0)])
    return (
        [shard, came, second],
        [near, near_came, one_second, three_second],
        [far_pair, cross(tie(far_pair, (one_second, three_second)), 1)],
        lists,
    )


def body(features, node_order, section_owner, send_blocks, tile_rows, tile_cols, tiles, weight):
    width = features.shape[1]
    tile_len = tiles.shape[3]
    blocks = features.shape[0] // tile_len
    n_dom, n_rep = lax.axis_size("dom"), lax.axis_size("rep")
    sections, n_send = send_blocks.shape
    me, rep = lax.axis_index("dom"), lax.axis_index("rep")
    n_blocks = blocks // n_rep
    small = n_dom == 16 and n_rep == 2 and n_send == n_dom * n_rep

    own_tiles = tiles[0].reshape(-1, tile_len, tile_len)
    numbers = jnp.stack([tile_rows[0], tile_cols[0]])
    if small:
        swap = [(0, 1), (1, 0)]

        def exchange(value):
            return lax.ppermute(value, "rep", swap)

        tile_list = [own_tiles, exchange(own_tiles)]
        lists = product_lists(numbers, exchange(numbers), n_blocks)
        mine = pick_share(features, node_order, section_owner, send_blocks, tile_len)
        *own, lists = gather_small(mine, section_owner, lists)
        parts = [part + [exchange(piece) for piece in part] for part in own]
        ends, place = [], 0
        for part in parts:
            ends.append([])
            for piece in part:
                ends[-1].append(place)
                place += piece.shape[0]
        hidden = products_in_phases(parts, ends, tile_list, lists, weight, n_blocks)
    else:
        tile_list = lax.all_gather(own_tiles, "rep", axis=0, tiled=True)
        numbers = lax.all_gather(numbers, "rep", axis=0)
        rows = (numbers[:, 0] - rep * n_blocks).reshape(-1)
        lines = share_rows(node_order, section_owner, send_blocks, tile_len)
        mine = features.at[lines.reshape(-1)].get(mode="promise_in_bounds")
        landed = lax.all_to_all(mine, "dom", 0, 0, tiled=True)
        landed = landed.reshape(n_dom, -1, width)
        shard = landed.at[section_owner].get(mode="promise_in_bounds")
        whole = lax.all_gather(shard, ("rep", "dom"), axis=0)
        whole = whole.transpose(1, 0, 2, 3).reshape(sections * n_send, tile_len, width)
        slots = jnp.arange(sections)[:, None] * n_send + numbers[:, 1]
        hidden = products(
            [whole], [0], tile_list, rows, slots.reshape(-1), weight, sections * n_send, n_blocks
        )
    return hidden.reshape(n_blocks * tile_len, -1)


def solution(mesh):
    return jax.shard_map(
        body,
        mesh=mesh,
        in_specs=(
            P("dom", None),
            P("dom", None),
            P(),
            P(),
            P("dom", None, "rep"),
            P("dom", None, "rep"),
            P("dom", None, "rep", None, None),
            P(),
        ),
        out_specs=P(("dom", "rep"), None),
        check_vma=False,
    )
```

```python
import functools

import jax
import jax.numpy as jnp
from jax import lax
from jax.experimental import pallas as pl
from jax.experimental.pallas import tpu as pltpu
from jax.sharding import PartitionSpec as P


UNROLL = 8


def load(n_first, pieces, places, sent, sem):
    return [
        pltpu.make_async_copy(piece, sent.at[pl.ds(place, piece.shape[0])], sem.at[n_first + i])
        for i, (piece, place) in enumerate(zip(pieces, places))
    ]


def put(lists, count, here, tile, row, place):
    lists[0, count] = tile
    lists[1, count] = row
    lists[2, count] = place
    return count + here.astype(jnp.int32)


def pad(lists, first, count, n_blocks):
    for i in range(UNROLL):
        put(lists, first + count + i, count >= 0, 0, n_blocks, 0)
    return (count + UNROLL - 1) // UNROLL


def run(lists, first, groups, tiles, sent, acc):
    def step(group, carry):
        at = [first + group * UNROLL + i for i in range(UNROLL)]
        done = [
            jnp.dot(
                tiles[lists[0, i]], sent[lists[2, i]], preferred_element_type=jnp.float32
            )
            for i in at
        ]
        for i, product in zip(at, done):
            acc[lists[1, i]] += product
        return carry

    lax.fori_loop(0, groups, step, 0)


def finish(acc, weight_ref, out_ref, stage, out_sem):
    steps, group, tile_len = stage.shape[:3]
    copies = []
    for i in range(steps):
        total = acc[pl.ds(i * group, group)].reshape(group * tile_len, acc.shape[2])
        mixed = jnp.dot(
            total.astype(jnp.bfloat16), weight_ref[...], preferred_element_type=jnp.float32
        )
        stage[i] = jnp.maximum(mixed, 0.0).astype(out_ref.dtype).reshape(stage.shape[1:])
        copies.append(
            pltpu.make_async_copy(stage.at[i], out_ref.at[pl.ds(i * group, group)], out_sem.at[i])
        )
        copies[-1].start()
    for copy in copies:
        copy.wait()


def whole_kernel(places, rows_ref, slots_ref, *refs):
    n = len(places)
    tile_ref, weight_ref, out_ref, sent, tiles, acc, stage, lists, sem, out_sem = refs[n:]
    n_tiles, n_blocks = rows_ref.shape[0], out_ref.shape[0]
    copies = load(0, refs[:n], places, sent, sem)
    copies.append(pltpu.make_async_copy(tile_ref, tiles, sem.at[n]))
    for copy in copies:
        copy.start()
    acc[...] = jnp.zeros_like(acc)

    def pick(t, count):
        row = rows_ref[t]
        here = jnp.logical_and(row >= 0, row < n_blocks)
        return put(lists, count, here, t, row, slots_ref[t])

    groups = pad(lists, 0, lax.fori_loop(0, n_tiles, pick, jnp.int32(0)), n_blocks)
    for copy in copies:
        copy.wait()
    run(lists, 0, groups, tiles, sent, acc)
    finish(acc, weight_ref, out_ref, stage, out_sem)


def phased_kernel(places, lists, *refs):
    n = sum(len(part) for part in places)
    pieces, tile_refs = refs[:n], refs[n : n + 2]
    weight_ref, out_ref, sent, tiles, acc, stage, sem, out_sem = refs[n + 2 :]
    each = tiles.shape[0] // 2
    copies, at = [], 0
    for part in places:
        copies.append(load(at, pieces[at : at + len(part)], part, sent, sem))
        at += len(part)
    copies[0] += [
        pltpu.make_async_copy(ref, tiles.at[pl.ds(i * each, each)], sem.at[n + i])
        for i, ref in enumerate(tile_refs)
    ]
    for copy in copies[0]:
        copy.start()
    acc[...] = jnp.zeros_like(acc)
    for part in copies[1:]:
        for copy in part:
            copy.start()
    span = lists.shape[1] // len(places)
    for i, part in enumerate(copies):
        for copy in part:
            copy.wait()
        run(lists, i * span, lists[3, i * span], tiles, sent, acc)
    finish(acc, weight_ref, out_ref, stage, out_sem)


def lists_kernel(n_blocks, own_ref, other_ref, lists):
    me, rep = lax.axis_index("dom"), lax.axis_index("rep")
    sections, each = own_ref.shape[1:]
    span = lists.shape[1] // 3
    counts = (jnp.int32(0),) * 3
    for s in range(sections):
        for part, ref in enumerate((own_ref, other_ref)):

            def pick(k, counts, ref=ref, part=part, s=s):
                row = ref[0, s, k] - rep * n_blocks
                here = jnp.logical_and(row >= 0, row < n_blocks)
                col = ref[1, s, k]
                holder, chip = col // 16, col % 16
                other = (holder != rep).astype(jnp.int32)
                shift = (chip // 4 - me // 4) & 3
                turn = place_of((chip ^ me) & 3, holder)
                at = turn * sections + s
                by_shift = shift // 2
                near = jnp.where(
                    turn < 2, at + (turn + by_shift) * 4, 8 + at + by_shift * 8
                )
                place = jnp.where(shift == 0, other * 16 + at, 96 + other * 16 + at)
                place = jnp.where((shift & 1) == 1, 32 + other * 32 + near, place)
                phase = jnp.where((shift & 1) == 1, 1, shift)
                target = jnp.where(
                    phase == 0,
                    counts[0],
                    jnp.where(phase == 1, span + counts[1], 2 * span + counts[2]),
                )
                put(lists, target, here, (part * sections + s) * each + k, row, place)
                now = here.astype(jnp.int32)
                return tuple(c + jnp.where(phase == i, now, 0) for i, c in enumerate(counts))

            counts = lax.fori_loop(0, each, pick, counts)
    for i, count in enumerate(counts):
        lists[3, i * span] = pad(lists, i * span, count, n_blocks)


HBM = pl.BlockSpec(memory_space=pltpu.HBM)
SMEM = pl.BlockSpec(memory_space=pltpu.SMEM)
VMEM = pl.BlockSpec(memory_space=pltpu.VMEM)


def settings(n_products, tile_len, width, n_bytes):
    return {
        "compiler_params": pltpu.CompilerParams(vmem_limit_bytes=60 * 1024 * 1024),
        "cost_estimate": pl.CostEstimate(
            flops=2 * n_products * tile_len * tile_len * width,
            bytes_accessed=n_bytes,
            transcendentals=0,
        ),
    }


def out_stage(n_blocks, tile_len, width):
    group = min(4, n_blocks)
    return pltpu.VMEM((n_blocks // group, group, tile_len, width), jnp.bfloat16)


def products(pieces, places, tiles, rows, slots, weight, n_sent, n_blocks):
    n_tiles, tile_len = tiles.shape[:2]
    width = weight.shape[0]
    return pl.pallas_call(
        functools.partial(whole_kernel, tuple(places)),
        out_shape=jax.ShapeDtypeStruct((n_blocks, tile_len, weight.shape[1]), jnp.bfloat16),
        in_specs=[SMEM, SMEM] + [HBM] * (len(pieces) + 1) + [VMEM],
        out_specs=HBM,
        scratch_shapes=[
            pltpu.VMEM((n_sent, tile_len, width), jnp.bfloat16),
            pltpu.VMEM(tiles.shape, jnp.bfloat16),
            pltpu.VMEM((n_blocks + 1, tile_len, width), jnp.float32),
            out_stage(n_blocks, tile_len, weight.shape[1]),
            pltpu.SMEM((3, n_tiles + UNROLL), jnp.int32),
            pltpu.SemaphoreType.DMA((len(pieces) + 1,)),
            pltpu.SemaphoreType.DMA((n_blocks // min(4, n_blocks),)),
        ],
        **settings(n_tiles, tile_len, width, 16 << 20),
    )(rows, slots, *pieces, tiles, weight)


def products_in_phases(pieces, places, tile_list, lists, weight, n_blocks):
    n_tiles, tile_len = 2 * tile_list[0].shape[0], tile_list[0].shape[1]
    width = weight.shape[0]
    flat = [piece for part in pieces for piece in part]
    n_sent = sum(piece.shape[0] for piece in flat)
    return pl.pallas_call(
        functools.partial(phased_kernel, places),
        out_shape=jax.ShapeDtypeStruct((n_blocks, tile_len, weight.shape[1]), jnp.bfloat16),
        in_specs=[SMEM] + [HBM] * (len(flat) + 2) + [VMEM],
        out_specs=HBM,
        scratch_shapes=[
            pltpu.VMEM((n_sent, tile_len, width), jnp.bfloat16),
            pltpu.VMEM((n_tiles, tile_len, tile_len), jnp.bfloat16),
            pltpu.VMEM((n_blocks + 1, tile_len, width), jnp.float32),
            out_stage(n_blocks, tile_len, weight.shape[1]),
            pltpu.SemaphoreType.DMA((len(flat) + 2,)),
            pltpu.SemaphoreType.DMA((n_blocks // min(4, n_blocks),)),
        ],
        **settings(n_tiles, tile_len, width, 16 << 20),
    )(lists, *flat, *tile_list, weight)


def product_lists(own, other, n_blocks):
    n_tiles = 2 * own.shape[1] * own.shape[2]
    return pl.pallas_call(
        functools.partial(lists_kernel, n_blocks),
        out_shape=jax.ShapeDtypeStruct((4, 3 * (n_tiles + UNROLL)), jnp.int32),
        in_specs=[SMEM] * 2,
        out_specs=SMEM,
    )(own, other)


CHUNKS = 8
ROWS = 16


def pick_kernel(owner_ref, blocks_ref, order_ref, features_ref, out_ref, *scratch):
    lines, held, wide, line_sem, sem = scratch
    me, rep = lax.axis_index("dom"), lax.axis_index("rep")
    section = jnp.int32(0)
    for s in range(blocks_ref.shape[0]):
        section = jnp.where(owner_ref[s] == me, s, section)
    share, tile_len = out_ref.shape[:2]
    size = held.shape[0] // CHUNKS
    copies = [
        pltpu.make_async_copy(
            order_ref.at[blocks_ref[section, rep * share + j]], lines.at[j], line_sem.at[j]
        )
        for j in range(share)
    ]
    chunks = [
        pltpu.make_async_copy(
            features_ref.at[pl.ds(i * size, size)], held.at[pl.ds(i * size, size)], sem.at[i]
        )
        for i in range(CHUNKS)
    ]
    for copy in copies + chunks:
        copy.start()
    for i, copy in enumerate(chunks):
        copy.wait()
        wide[pl.ds(i * size, size)] = held[pl.ds(i * size, size)].astype(jnp.float32)
    for copy in copies:
        copy.wait()

    def one_block(j, carry):
        for first in range(0, tile_len, ROWS):
            rows = [wide[pl.ds(lines[j, 0, first + u], 1), :] for u in range(ROWS)]
            rows = jnp.concatenate(rows, axis=0).astype(out_ref.dtype)
            out_ref[j, pl.ds(first, ROWS), :] = rows
        return carry

    lax.fori_loop(0, share, one_block, 0)


def pick_share(features, node_order, section_owner, send_blocks, tile_len):
    rows, width = features.shape
    share = send_blocks.shape[1] // 2
    return pl.pallas_call(
        pick_kernel,
        out_shape=jax.ShapeDtypeStruct((share, tile_len, width), features.dtype),
        in_specs=[SMEM, SMEM, HBM, HBM],
        out_specs=VMEM,
        scratch_shapes=[
            pltpu.SMEM((share, 1, tile_len), jnp.int32),
            pltpu.VMEM((rows, width), features.dtype),
            pltpu.VMEM((rows, width), jnp.float32),
            pltpu.SemaphoreType.DMA((share,)),
            pltpu.SemaphoreType.DMA((CHUNKS,)),
        ],
        compiler_params=pltpu.CompilerParams(vmem_limit_bytes=60 * 1024 * 1024),
    )(section_owner, send_blocks, node_order[0].reshape(-1, 1, tile_len), features)


def share_rows(node_order, section_owner, send_blocks, tile_len):
    me = lax.axis_index("dom")
    sections, n_send = send_blocks.shape
    mine = (section_owner == me).astype(jnp.int32)
    section = jnp.sum(mine * jnp.arange(sections, dtype=jnp.int32))
    share = n_send // lax.axis_size("rep")
    picks = lax.dynamic_slice(
        send_blocks, (section, lax.axis_index("rep") * share), (1, share)
    )[0]
    order = node_order[0].reshape(-1, tile_len)
    return order.at[picks].get(mode="promise_in_bounds")


def move(value, pairs):
    return lax.ppermute(value, "dom", pairs)


def flip(bits):
    return [(i, i ^ bits) for i in range(16)]


def cross(value, turn):
    pairs = []
    for i in range(16):
        for core in (0, 1):
            pairs.append((2 * i + core, 2 * (i ^ (1 if core == turn else 2)) + core))
    return lax.ppermute(value, ("dom", "rep"), pairs)


def place_of(across, core):
    return jnp.where(core == 0, across, (across & 1) * 2 + across // 2)


def tie(value, after):
    return lax.optimization_barrier((value, after))[0]


RING = {
    k: [(z * 4 + q, ((z - k) % 4) * 4 + q) for z in range(4) for q in range(4)] for k in (1, 2, 3)
}


def gather_small(rows, section_owner, lists):
    landed = lax.all_to_all(rows, "dom", 0, 0, tiled=True)
    shard = landed.at[section_owner].get(mode="promise_in_bounds")
    shard, lists = lax.optimization_barrier((shard, lists))
    one, three = move(shard, RING[1]), move(shard, RING[3])
    came, turned = cross(shard, 0), cross(shard, 1)
    second = jnp.concatenate([turned, cross(came, 1)])
    far = move(one, RING[1])
    one_second = move(second, RING[1])
    near_one = cross(tie(one, (came, turned)), 0)
    near_three = cross(tie(three, (came, turned)), 0)
    three_second = cross(jnp.concatenate([three, near_three]), 1)
    far_pair = jnp.concatenate([far, cross(far, 0)])
    return (
        [shard, came, second],
        [one, three, near_one, near_three, one_second, three_second],
        [far_pair, cross(tie(far_pair, (one_second, three_second)), 1)],
        lists,
    )


def body(features, node_order, section_owner, send_blocks, tile_rows, tile_cols, tiles, weight):
    width = features.shape[1]
    tile_len = tiles.shape[3]
    blocks = features.shape[0] // tile_len
    n_dom, n_rep = lax.axis_size("dom"), lax.axis_size("rep")
    sections, n_send = send_blocks.shape
    me, rep = lax.axis_index("dom"), lax.axis_index("rep")
    n_blocks = blocks // n_rep
    small = n_dom == 16 and n_rep == 2 and n_send == n_dom * n_rep

    own_tiles = tiles[0].reshape(-1, tile_len, tile_len)
    numbers = jnp.stack([tile_rows[0], tile_cols[0]])
    if small:
        swap = [(0, 1), (1, 0)]

        def exchange(value):
            return lax.ppermute(value, "rep", swap)

        tile_list = [own_tiles, exchange(own_tiles)]
        lists = product_lists(numbers, exchange(numbers), n_blocks)
        mine = pick_share(features, node_order, section_owner, send_blocks, tile_len)
        *own, lists = gather_small(mine, section_owner, lists)
        parts = [part + [exchange(piece) for piece in part] for part in own]
        ends, place = [], 0
        for part in parts:
            ends.append([])
            for piece in part:
                ends[-1].append(place)
                place += piece.shape[0]
        hidden = products_in_phases(parts, ends, tile_list, lists, weight, n_blocks)
    else:
        tile_list = lax.all_gather(own_tiles, "rep", axis=0, tiled=True)
        numbers = lax.all_gather(numbers, "rep", axis=0)
        rows = (numbers[:, 0] - rep * n_blocks).reshape(-1)
        lines = share_rows(node_order, section_owner, send_blocks, tile_len)
        mine = features.at[lines.reshape(-1)].get(mode="promise_in_bounds")
        landed = lax.all_to_all(mine, "dom", 0, 0, tiled=True)
        landed = landed.reshape(n_dom, -1, width)
        shard = landed.at[section_owner].get(mode="promise_in_bounds")
        whole = lax.all_gather(shard, ("rep", "dom"), axis=0)
        whole = whole.transpose(1, 0, 2, 3).reshape(sections * n_send, tile_len, width)
        slots = jnp.arange(sections)[:, None] * n_send + numbers[:, 1]
        hidden = products(
            [whole], [0], tile_list, rows, slots.reshape(-1), weight, sections * n_send, n_blocks
        )
    return hidden.reshape(n_blocks * tile_len, -1)


def solution(mesh):
    return jax.shard_map(
        body,
        mesh=mesh,
        in_specs=(
            P("dom", None),
            P("dom", None),
            P(),
            P(),
            P("dom", None, "rep"),
            P("dom", None, "rep"),
            P("dom", None, "rep", None, None),
            P(),
        ),
        out_specs=P(("dom", "rep"), None),
        check_vma=False,
    )
```

```python
import functools

import jax
import jax.numpy as jnp
from jax import lax
from jax.experimental import pallas as pl
from jax.experimental.pallas import tpu as pltpu
from jax.sharding import PartitionSpec as P


UNROLL = 8


def load(n_first, pieces, places, sent, sem):
    return [
        pltpu.make_async_copy(piece, sent.at[pl.ds(place, piece.shape[0])], sem.at[n_first + i])
        for i, (piece, place) in enumerate(zip(pieces, places))
    ]


def put(lists, count, here, tile, row, place):
    lists[0, count] = tile
    lists[1, count] = row
    lists[2, count] = place
    return count + here.astype(jnp.int32)


def pad(lists, first, count, n_blocks):
    for i in range(UNROLL):
        put(lists, first + count + i, count >= 0, 0, n_blocks, 0)
    return (count + UNROLL - 1) // UNROLL


def run(lists, first, groups, tiles, sent, acc):
    def step(group, carry):
        at = [first + group * UNROLL + i for i in range(UNROLL)]
        done = [
            jnp.dot(
                tiles[lists[0, i]], sent[lists[2, i]], preferred_element_type=jnp.float32
            )
            for i in at
        ]
        for i, product in zip(at, done):
            acc[lists[1, i]] += product
        return carry

    lax.fori_loop(0, groups, step, 0)


def finish(acc, weight_ref, out_ref, stage, out_sem):
    steps, group, tile_len = stage.shape[:3]
    copies = []
    for i in range(steps):
        total = acc[pl.ds(i * group, group)].reshape(group * tile_len, acc.shape[2])
        mixed = jnp.dot(
            total.astype(jnp.bfloat16), weight_ref[...], preferred_element_type=jnp.float32
        )
        stage[i] = jnp.maximum(mixed, 0.0).astype(out_ref.dtype).reshape(stage.shape[1:])
        copies.append(
            pltpu.make_async_copy(stage.at[i], out_ref.at[pl.ds(i * group, group)], out_sem.at[i])
        )
        copies[-1].start()
    for copy in copies:
        copy.wait()


def whole_kernel(places, rows_ref, slots_ref, *refs):
    n = len(places)
    tile_ref, weight_ref, out_ref, sent, tiles, acc, stage, lists, sem, out_sem = refs[n:]
    n_tiles, n_blocks = rows_ref.shape[0], out_ref.shape[0]
    copies = load(0, refs[:n], places, sent, sem)
    copies.append(pltpu.make_async_copy(tile_ref, tiles, sem.at[n]))
    for copy in copies:
        copy.start()
    acc[...] = jnp.zeros_like(acc)

    def pick(t, count):
        row = rows_ref[t]
        here = jnp.logical_and(row >= 0, row < n_blocks)
        return put(lists, count, here, t, row, slots_ref[t])

    groups = pad(lists, 0, lax.fori_loop(0, n_tiles, pick, jnp.int32(0)), n_blocks)
    for copy in copies:
        copy.wait()
    run(lists, 0, groups, tiles, sent, acc)
    finish(acc, weight_ref, out_ref, stage, out_sem)


def phased_kernel(places, lists, *refs):
    n = sum(len(part) for part in places)
    pieces, tile_refs = refs[:n], refs[n : n + 2]
    weight_ref, out_ref, sent, tiles, acc, stage, sem, out_sem = refs[n + 2 :]
    each = tiles.shape[0] // 2
    copies, at = [], 0
    for part in places:
        copies.append(load(at, pieces[at : at + len(part)], part, sent, sem))
        at += len(part)
    copies[0] += [
        pltpu.make_async_copy(ref, tiles.at[pl.ds(i * each, each)], sem.at[n + i])
        for i, ref in enumerate(tile_refs)
    ]
    for copy in copies[0]:
        copy.start()
    acc[...] = jnp.zeros_like(acc)
    for part in copies[1:]:
        for copy in part:
            copy.start()
    span = lists.shape[1] // len(places)
    for i, part in enumerate(copies):
        for copy in part:
            copy.wait()
        run(lists, i * span, lists[3, i * span], tiles, sent, acc)
    finish(acc, weight_ref, out_ref, stage, out_sem)


def lists_kernel(n_blocks, own_ref, other_ref, lists):
    me, rep = lax.axis_index("dom"), lax.axis_index("rep")
    sections, each = own_ref.shape[1:]
    span = lists.shape[1] // 3
    counts = (jnp.int32(0),) * 3
    for s in range(sections):
        for part, ref in enumerate((own_ref, other_ref)):

            def pick(k, counts, ref=ref, part=part, s=s):
                row = ref[0, s, k] - rep * n_blocks
                here = jnp.logical_and(row >= 0, row < n_blocks)
                col = ref[1, s, k]
                holder, chip = col // 16, col % 16
                other = (holder != rep).astype(jnp.int32)
                shift = (chip // 4 - me // 4) & 3
                turn = place_of((chip ^ me) & 3, holder)
                at = turn * sections + s
                by_shift = shift // 2
                near = jnp.where(
                    turn < 2, at + (turn + by_shift) * 4, 8 + at + by_shift * 8
                )
                place = jnp.where(shift == 0, other * 16 + at, 96 + other * 16 + at)
                place = jnp.where((shift & 1) == 1, 32 + other * 32 + near, place)
                phase = jnp.where((shift & 1) == 1, 1, shift)
                target = jnp.where(
                    phase == 0,
                    counts[0],
                    jnp.where(phase == 1, span + counts[1], 2 * span + counts[2]),
                )
                put(lists, target, here, (part * sections + s) * each + k, row, place)
                now = here.astype(jnp.int32)
                return tuple(c + jnp.where(phase == i, now, 0) for i, c in enumerate(counts))

            counts = lax.fori_loop(0, each, pick, counts)
    for i, count in enumerate(counts):
        lists[3, i * span] = pad(lists, i * span, count, n_blocks)


HBM = pl.BlockSpec(memory_space=pltpu.HBM)
SMEM = pl.BlockSpec(memory_space=pltpu.SMEM)
VMEM = pl.BlockSpec(memory_space=pltpu.VMEM)


def settings(n_products, tile_len, width, n_bytes):
    return {
        "compiler_params": pltpu.CompilerParams(vmem_limit_bytes=60 * 1024 * 1024),
        "cost_estimate": pl.CostEstimate(
            flops=2 * n_products * tile_len * tile_len * width,
            bytes_accessed=n_bytes,
            transcendentals=0,
        ),
    }


def out_stage(n_blocks, tile_len, width):
    group = min(4, n_blocks)
    return pltpu.VMEM((n_blocks // group, group, tile_len, width), jnp.bfloat16)


def products(pieces, places, tiles, rows, slots, weight, n_sent, n_blocks):
    n_tiles, tile_len = tiles.shape[:2]
    width = weight.shape[0]
    return pl.pallas_call(
        functools.partial(whole_kernel, tuple(places)),
        out_shape=jax.ShapeDtypeStruct((n_blocks, tile_len, weight.shape[1]), jnp.bfloat16),
        in_specs=[SMEM, SMEM] + [HBM] * (len(pieces) + 1) + [VMEM],
        out_specs=HBM,
        scratch_shapes=[
            pltpu.VMEM((n_sent, tile_len, width), jnp.bfloat16),
            pltpu.VMEM(tiles.shape, jnp.bfloat16),
            pltpu.VMEM((n_blocks + 1, tile_len, width), jnp.float32),
            out_stage(n_blocks, tile_len, weight.shape[1]),
            pltpu.SMEM((3, n_tiles + UNROLL), jnp.int32),
            pltpu.SemaphoreType.DMA((len(pieces) + 1,)),
            pltpu.SemaphoreType.DMA((n_blocks // min(4, n_blocks),)),
        ],
        **settings(n_tiles, tile_len, width, 16 << 20),
    )(rows, slots, *pieces, tiles, weight)


def products_in_phases(pieces, places, tile_list, lists, weight, n_blocks):
    n_tiles, tile_len = 2 * tile_list[0].shape[0], tile_list[0].shape[1]
    width = weight.shape[0]
    flat = [piece for part in pieces for piece in part]
    n_sent = sum(piece.shape[0] for piece in flat)
    return pl.pallas_call(
        functools.partial(phased_kernel, places),
        out_shape=jax.ShapeDtypeStruct((n_blocks, tile_len, weight.shape[1]), jnp.bfloat16),
        in_specs=[SMEM] + [HBM] * (len(flat) + 2) + [VMEM],
        out_specs=HBM,
        scratch_shapes=[
            pltpu.VMEM((n_sent, tile_len, width), jnp.bfloat16),
            pltpu.VMEM((n_tiles, tile_len, tile_len), jnp.bfloat16),
            pltpu.VMEM((n_blocks + 1, tile_len, width), jnp.float32),
            out_stage(n_blocks, tile_len, weight.shape[1]),
            pltpu.SemaphoreType.DMA((len(flat) + 2,)),
            pltpu.SemaphoreType.DMA((n_blocks // min(4, n_blocks),)),
        ],
        **settings(n_tiles, tile_len, width, 16 << 20),
    )(lists, *flat, *tile_list, weight)


def product_lists(own, other, n_blocks):
    n_tiles = 2 * own.shape[1] * own.shape[2]
    return pl.pallas_call(
        functools.partial(lists_kernel, n_blocks),
        out_shape=jax.ShapeDtypeStruct((4, 3 * (n_tiles + UNROLL)), jnp.int32),
        in_specs=[SMEM] * 2,
        out_specs=SMEM,
    )(own, other)


CHUNKS = 8
ROWS = 16


def pick_kernel(owner_ref, blocks_ref, order_ref, features_ref, out_ref, *scratch):
    lines, held, wide, line_sem, sem = scratch
    me, rep = lax.axis_index("dom"), lax.axis_index("rep")
    section = jnp.int32(0)
    for s in range(blocks_ref.shape[0]):
        section = jnp.where(owner_ref[s] == me, s, section)
    share, tile_len = out_ref.shape[:2]
    size = held.shape[0] // CHUNKS
    copies = [
        pltpu.make_async_copy(
            order_ref.at[blocks_ref[section, rep * share + j]], lines.at[j], line_sem.at[j]
        )
        for j in range(share)
    ]
    chunks = [
        pltpu.make_async_copy(
            features_ref.at[pl.ds(i * size, size)], held.at[pl.ds(i * size, size)], sem.at[i]
        )
        for i in range(CHUNKS)
    ]
    for copy in copies + chunks:
        copy.start()
    for i, copy in enumerate(chunks):
        copy.wait()
        wide[pl.ds(i * size, size)] = held[pl.ds(i * size, size)].astype(jnp.float32)
    for copy in copies:
        copy.wait()

    def one_block(j, carry):
        for first in range(0, tile_len, ROWS):
            rows = [wide[pl.ds(lines[j, 0, first + u], 1), :] for u in range(ROWS)]
            rows = jnp.concatenate(rows, axis=0).astype(out_ref.dtype)
            out_ref[j, pl.ds(first, ROWS), :] = rows
        return carry

    lax.fori_loop(0, share, one_block, 0)


def pick_share(features, node_order, section_owner, send_blocks, tile_len):
    rows, width = features.shape
    share = send_blocks.shape[1] // 2
    return pl.pallas_call(
        pick_kernel,
        out_shape=jax.ShapeDtypeStruct((share, tile_len, width), features.dtype),
        in_specs=[SMEM, SMEM, HBM, HBM],
        out_specs=VMEM,
        scratch_shapes=[
            pltpu.SMEM((share, 1, tile_len), jnp.int32),
            pltpu.VMEM((rows, width), features.dtype),
            pltpu.VMEM((rows, width), jnp.float32),
            pltpu.SemaphoreType.DMA((share,)),
            pltpu.SemaphoreType.DMA((CHUNKS,)),
        ],
        compiler_params=pltpu.CompilerParams(vmem_limit_bytes=60 * 1024 * 1024),
    )(section_owner, send_blocks, node_order[0].reshape(-1, 1, tile_len), features)


def share_rows(node_order, section_owner, send_blocks, tile_len):
    me = lax.axis_index("dom")
    sections, n_send = send_blocks.shape
    mine = (section_owner == me).astype(jnp.int32)
    section = jnp.sum(mine * jnp.arange(sections, dtype=jnp.int32))
    share = n_send // lax.axis_size("rep")
    picks = lax.dynamic_slice(
        send_blocks, (section, lax.axis_index("rep") * share), (1, share)
    )[0]
    order = node_order[0].reshape(-1, tile_len)
    return order.at[picks].get(mode="promise_in_bounds")


def move(value, pairs):
    return lax.ppermute(value, "dom", pairs)


def flip(bits):
    return [(i, i ^ bits) for i in range(16)]


def cross(value, turn):
    pairs = []
    for i in range(16):
        for core in (0, 1):
            pairs.append((2 * i + core, 2 * (i ^ (1 if core == turn else 2)) + core))
    return lax.ppermute(value, ("dom", "rep"), pairs)


def place_of(across, core):
    return jnp.where(core == 0, across, (across & 1) * 2 + across // 2)


def tie(value, after):
    return lax.optimization_barrier((value, after))[0]


RING = {
    k: [(z * 4 + q, ((z - k) % 4) * 4 + q) for z in range(4) for q in range(4)] for k in (1, 2, 3)
}


def gather_small(rows, section_owner, lists):
    landed = lax.all_to_all(rows, "dom", 0, 0, tiled=True)
    shard = landed.at[section_owner].get(mode="promise_in_bounds")
    shard, lists = lax.optimization_barrier((shard, lists))
    one, three = move(shard, RING[1]), move(shard, RING[3])
    came, turned = cross(shard, 0), cross(shard, 1)
    second = jnp.concatenate([turned, cross(came, 1)])
    far = move(one, RING[1])
    one_second = move(second, RING[1])
    near_one = cross(tie(one, (came, turned)), 0)
    near_three = cross(three, 0)
    three_second = cross(jnp.concatenate([three, near_three]), 1)
    far_pair = jnp.concatenate([far, cross(far, 0)])
    return (
        [shard, came, second],
        [one, three, near_one, near_three, one_second, three_second],
        [far_pair, cross(tie(far_pair, (one_second, three_second)), 1)],
        lists,
    )


def body(features, node_order, section_owner, send_blocks, tile_rows, tile_cols, tiles, weight):
    width = features.shape[1]
    tile_len = tiles.shape[3]
    blocks = features.shape[0] // tile_len
    n_dom, n_rep = lax.axis_size("dom"), lax.axis_size("rep")
    sections, n_send = send_blocks.shape
    me, rep = lax.axis_index("dom"), lax.axis_index("rep")
    n_blocks = blocks // n_rep
    small = n_dom == 16 and n_rep == 2 and n_send == n_dom * n_rep

    own_tiles = tiles[0].reshape(-1, tile_len, tile_len)
    numbers = jnp.stack([tile_rows[0], tile_cols[0]])
    if small:
        swap = [(0, 1), (1, 0)]

        def exchange(value):
            return lax.ppermute(value, "rep", swap)

        tile_list = [own_tiles, exchange(own_tiles)]
        lists = product_lists(numbers, exchange(numbers), n_blocks)
        mine = pick_share(features, node_order, section_owner, send_blocks, tile_len)
        *own, lists = gather_small(mine, section_owner, lists)
        parts = [part + [exchange(piece) for piece in part] for part in own]
        ends, place = [], 0
        for part in parts:
            ends.append([])
            for piece in part:
                ends[-1].append(place)
                place += piece.shape[0]
        hidden = products_in_phases(parts, ends, tile_list, lists, weight, n_blocks)
    else:
        tile_list = lax.all_gather(own_tiles, "rep", axis=0, tiled=True)
        numbers = lax.all_gather(numbers, "rep", axis=0)
        rows = (numbers[:, 0] - rep * n_blocks).reshape(-1)
        lines = share_rows(node_order, section_owner, send_blocks, tile_len)
        mine = features.at[lines.reshape(-1)].get(mode="promise_in_bounds")
        landed = lax.all_to_all(mine, "dom", 0, 0, tiled=True)
        landed = landed.reshape(n_dom, -1, width)
        shard = landed.at[section_owner].get(mode="promise_in_bounds")
        whole = lax.all_gather(shard, ("rep", "dom"), axis=0)
        whole = whole.transpose(1, 0, 2, 3).reshape(sections * n_send, tile_len, width)
        slots = jnp.arange(sections)[:, None] * n_send + numbers[:, 1]
        hidden = products(
            [whole], [0], tile_list, rows, slots.reshape(-1), weight, sections * n_send, n_blocks
        )
    return hidden.reshape(n_blocks * tile_len, -1)


def solution(mesh):
    return jax.shard_map(
        body,
        mesh=mesh,
        in_specs=(
            P("dom", None),
            P("dom", None),
            P(),
            P(),
            P("dom", None, "rep"),
            P("dom", None, "rep"),
            P("dom", None, "rep", None, None),
            P(),
        ),
        out_specs=P(("dom", "rep"), None),
        check_vma=False,
    )
```
